256 devices in a mesh: seq: 32 (over x, z), node: 4 (over y), dev: 2 (over core).
Axes of the slice: x: 4, y: 4, z: 8, core: 2. Of those that a mesh axis runs over, the one named last changes fastest.
Arguments:
- hidden: bfloat16 [8, 4096, 4096], P(('node', 'dev'), None, 'seq'), may hold values from -6 to 6
- out_grad: bfloat16 [8, 4096, 4096], P(('node', 'dev'), None, 'seq'), may hold values from -6 to 6
- queries: bfloat16 [8, 4096, 2, 128], P(('node', 'dev'), 'seq'), may hold values from -6 to 6
- key_heads: bfloat16 [8, 4096, 128], P(('node', 'dev'), 'seq'), may hold values from -6 to 6
- value_heads: bfloat16 [8, 4096, 128], P(('node', 'dev'), 'seq'), may hold values from -6 to 6
- routes: int32 [8, 4096, 2], P(('node', 'dev')), may hold values from 0 to 127, all different within a row; in each aligned block of 128 rows (0 to 127, 128 to 255, ..., all dimensions but the last counted through in order) at most 3 rows name the same one
- route_gates: float32 [8, 4096, 2], P(('node', 'dev'), 'seq'), may hold values from 0.05 to 0.5
- w_query: bfloat16 [128, 4096, 128], P(('node', 'dev'), 'seq'), may hold values from -0.09375 to 0.09375
- w_out: bfloat16 [128, 128, 4096], P(('node', 'dev'), None, 'seq'), may hold values from -0.5 to 0.5
- w_key: bfloat16 [4096, 128], P('seq'), may hold values from -0.09375 to 0.09375
- w_value: bfloat16 [4096, 128], P('seq'), may hold values from -0.09375 to 0.09375
Outputs:
- grad_hidden: bfloat16 [8, 4096, 4096], P(('node', 'dev'), None, 'seq')
- grad_wq: float32 [128, 4096, 128], P(('node', 'dev'), 'seq')
- grad_wo: float32 [128, 128, 4096], P(('node', 'dev'), None, 'seq')
- key_projection_gradient: float32 [4096, 128], P('seq')
- value_projection_gradient: float32 [4096, 128], P('seq')
The draws below stay inside these ranges and needn't reach their ends.
Inputs may be any that keep to these rules, and one draw needn't show every extreme that they name: A token names 2 different experts. In each block of 128 consecutive positions of one sequence no expert is named by more than 3 routes, and in some blocks one expert is named by exactly 3.
All inputs are finite; a program needn't handle non-finite values.
Results may differ from the reference program's by a relative error of at most 0.018.
Values may be sent and summed in bfloat16 or wider, within the bound.
No kernel may reach another device: no remote copies, remote signals or barrier semaphores. Data moves between devices by JAX's collectives and lax.ppermute only.
A program may use at most 128 MiB of HBM per device.

```python
import math
import jax
import jax.numpy as jnp
import numpy as np
from jax import lax

D = 4096
HD = 128
EXPERTS = 128
TOP = 2
POS_DEV = 128
LEN = 4096
SEQS = 8
CAP = 3


def draw_key_heads(key, part):
    key = jax.random.fold_in(key, 1)
    return jnp.clip(jax.random.normal(key, (SEQS, LEN, HD), jnp.float32), -4.5, 4.5).astype(jnp.bfloat16)


def draw_queries(key, part):
    key = jax.random.fold_in(key, 2)
    return jnp.clip(jax.random.normal(key, (SEQS, LEN, TOP, HD), jnp.float32), -4.5, 4.5).astype(jnp.bfloat16)


def levels(key, shape, shards, low, high):
    gain = 1.0
    for position, shards_of in shards:
        steps = jax.random.uniform(jax.random.fold_in(jax.random.fold_in(key, 6), position), (shards_of,), jnp.float32, low / len(shards), high / len(shards))
        gain = gain * jnp.repeat(jnp.exp(steps), shape[position] // shards_of).reshape((-1,) + (1,) * (len(shape) - 1 - position))
    return gain


def deal_out(key, own, number, rows, count, top, most, lean):
    sequence = jax.random.permutation(key, count)
    heavy_load, usual = load_shares(count, rows * top, most, lean, True), load_shares(count, rows * top, most, lean, False)
    places = jnp.arange(count)

    def named(sizes, rotation):
        used = int((sizes > 0).sum())
        fixed = max(1, used // 4)
        shifted = fixed + (places - fixed + rotation * (used - fixed)) % max(1, count - fixed)
        return jnp.zeros((count,), jnp.int32).at[sequence[jnp.where(places < fixed, places, shifted)]].set(jnp.asarray(sizes, jnp.int32))

    sizes = jnp.where(number % 4 == 0, named(heavy_load, number // 4), named(usual, number - number // 4 - 1))
    mixed = jax.random.permutation(jax.random.fold_in(own, 3), count)
    donor, receiver = mixed[0:count // 2 * 2:2], mixed[1:count // 2 * 2:2]
    slack = jnp.minimum(sizes[donor] - 1, most - sizes[receiver]) // 2
    slack = jnp.where((donor == sequence[0]) | (receiver == sequence[0]) | (sizes[receiver] == 0), 0, jnp.maximum(slack, 0))
    shifted = jax.random.randint(jax.random.fold_in(own, 4), (count // 2,), 0, 1 << 20) % (slack + 1)
    sizes = sizes.at[donor].add(-shifted).at[receiver].add(shifted)
    members = jnp.searchsorted(jnp.cumsum(sizes), jnp.arange(rows * top), side="right").astype(jnp.int32)
    grid = members.reshape(top, rows).T
    grid = grid[jax.random.permutation(jax.random.fold_in(own, 1), rows)]
    rotation = jax.random.randint(jax.random.fold_in(own, 2), (rows, 1), 0, top)
    return jnp.take_along_axis(grid, (jnp.arange(top)[None, :] + rotation) % top, axis=1)


def load_shares(number_of, total, limit, lean, full):
    loads = [(1 << 20) // math.isqrt(rank ** lean) + 1 for rank in range(1, number_of + 1)]
    largest = limit if full else min(limit, max(-(-total // number_of), total * loads[0] // sum(loads)))
    least = 1 if total - largest >= number_of - 1 else 0
    counts, spare = [largest] + [least] * (number_of - 1), total - largest - least * (number_of - 1)
    while spare > 0:
        movable = [i for i in range(1, number_of) if counts[i] < largest] or [i for i in range(1, number_of) if counts[i] < limit]
        mass, budget = sum([loads[i] for i in movable]), spare
        for i in movable:
            more = min(limit - counts[i], max(1, budget * loads[i] // mass), spare)
            counts[i] = counts[i] + more
            spare = spare - more
    return np.array(counts)


def bell_draw(own_key, shape, scale, most, cuts=(), kind=jnp.bfloat16):
    entries = jax.random.normal(own_key, shape, jnp.float32) * scale
    if len(cuts) > 0:
        entries = levels(own_key, shape, cuts, -0.22, 0.18) * entries
    return jnp.clip(entries, min=-most, max=most).astype(kind)


def setup_inputs(seed: int = 0) -> dict:
    keys = jax.random.split(jax.random.key(seed), 12)
    hidden = bell_draw(keys[0], (SEQS, LEN, D), 1.0, 6.0, ((0, 8), (2, 32)))
    out_grad = bell_draw(keys[1], (SEQS, LEN, D), 1.0, 6.0, ((0, 8), (2, 32)))
    queries = draw_queries(jax.random.fold_in(keys[11], 71), 0)
    key_heads = draw_key_heads(jax.random.fold_in(keys[11], 71), 0)
    value_heads = bell_draw(keys[4], (SEQS, LEN, HD), 1.0, 6.0, ((0, 8), (1, 32)))
    routes_keys = jax.random.split(jax.random.fold_in(keys[5], 1), SEQS * LEN // POS_DEV)
    routes_turns = jax.random.permutation(jax.random.fold_in(keys[5], 3), SEQS * LEN // POS_DEV)
    routes = jax.vmap(lambda own, number: deal_out(jax.random.fold_in(keys[5], 2), own, number, POS_DEV, EXPERTS, TOP, CAP, 1))(routes_keys, routes_turns).reshape((SEQS, LEN, TOP))
    route_gates = jnp.clip(jnp.exp(math.log(0.5) - 2.3025851 * jax.random.uniform(keys[6], (SEQS, LEN, TOP), jnp.float32) ** levels(keys[6], (SEQS, LEN, TOP), ((0, 8), (1, 32)), -0.2, 0.2)), 0.05, 0.5)
    w_query = bell_draw(keys[7], (EXPERTS, D, HD), D ** -0.5, 0.09375, ((0, 8), (1, 32)))
    w_out = bell_draw(keys[8], (EXPERTS, HD, D), HD ** -0.5, 0.5, ((0, 8), (2, 32)))
    w_key = bell_draw(keys[9], (D, HD), D ** -0.5, 0.09375, ((0, 32),))
    w_value = bell_draw(keys[10], (D, HD), D ** -0.5, 0.09375, ((0, 32),))
    return {"hidden": hidden, "out_grad": out_grad, "queries": queries, "key_heads": key_heads, "value_heads": value_heads, "routes": routes, "route_gates": route_gates, "w_query": w_query, "w_out": w_out, "w_key": w_key, "w_value": w_value}


def block_slots(route_table):
    n_blocks = LEN // POS_DEV
    flat_routes = route_table.reshape(n_blocks, POS_DEV * TOP)
    is_expert = (flat_routes[:, :, None] == jnp.arange(EXPERTS, dtype=jnp.int32)[None, None, :]).astype(jnp.int32)
    earlier = jnp.cumsum(is_expert, axis=1) - is_expert
    return lax.optimization_barrier(jnp.sum(earlier * is_expert, axis=2)).reshape(LEN, TOP)

def attend(query_rows, key_rows, value_rows, head_grad, gate_rows, start_pos):
    score_scale = 1.0 / math.sqrt(HD)
    flat_query = query_rows.reshape(-1, HD)
    n_query = flat_query.shape[0]
    query_pos = start_pos + jnp.arange(n_query, dtype=jnp.int32) // TOP
    key_pos = jnp.arange(key_rows.shape[0], dtype=jnp.int32)
    scores = jnp.dot(flat_query, key_rows.T, preferred_element_type=jnp.float32) * score_scale
    scores = jnp.where(key_pos[None, :] <= query_pos[:, None], scores, -jnp.inf)
    row_max = lax.optimization_barrier(jnp.max(scores, axis=1, keepdims=True))
    weights = jnp.exp(scores - row_max)
    probability = weights / lax.optimization_barrier(jnp.sum(weights, axis=1, keepdims=True))
    prob_bf = probability.astype(jnp.bfloat16)
    head_out = jnp.dot(prob_bf, value_rows, preferred_element_type=jnp.float32)
    gated_out = (gate_rows.reshape(-1, 1) * head_out).astype(jnp.bfloat16)
    grad_bf = head_grad.astype(jnp.bfloat16)
    value_sum = jnp.dot(prob_bf.T, grad_bf, preferred_element_type=jnp.float32)
    prob_grad = jnp.dot(grad_bf, value_rows.T, preferred_element_type=jnp.float32)
    row_delta = lax.optimization_barrier(jnp.sum(head_grad * head_out, axis=1, keepdims=True))
    score_grad = (probability * (prob_grad - row_delta)).astype(jnp.bfloat16)
    query_grad = (jnp.dot(score_grad, key_rows, preferred_element_type=jnp.float32) * score_scale).astype(jnp.bfloat16)
    key_sum = jnp.dot(score_grad.T, flat_query, preferred_element_type=jnp.float32) * score_scale
    return (query_grad, gated_out, key_sum, value_sum)

def reference(hidden, out_grad, queries, key_heads, value_heads, routes, route_gates, w_query, w_out, w_key, w_value):
    n_blocks = LEN // POS_DEV
    seq_ids = jnp.arange(SEQS, dtype=jnp.int32)[:, None, None]
    pos_ids = jnp.arange(LEN, dtype=jnp.int32)[None, :, None]
    top_ids = jnp.arange(TOP, dtype=jnp.int32)[None, None, :]
    slot_ids = jax.vmap(block_slots)(routes)
    place_ids = (((routes * SEQS + seq_ids) * n_blocks + pos_ids // POS_DEV) * CAP + slot_ids).reshape(-1)
    slot_span = SEQS * n_blocks * CAP
    token_ids = (seq_ids * (LEN + 1) + pos_ids + 0 * top_ids).reshape(-1).astype(jnp.int32)
    route_ids = (seq_ids * (LEN * TOP + 1) + pos_ids * TOP + top_ids).reshape(-1).astype(jnp.int32)
    tok_index = jnp.full((EXPERTS * slot_span,), LEN, jnp.int32).at[place_ids].set(token_ids).reshape(EXPERTS, slot_span)
    route_index = jnp.full((EXPERTS * slot_span,), LEN * TOP, jnp.int32).at[place_ids].set(route_ids).reshape(EXPERTS, slot_span)
    pad_rows = jnp.zeros((SEQS, 1, D), jnp.bfloat16)
    hid_rows = jnp.concatenate([hidden, pad_rows], axis=1).reshape(SEQS * (LEN + 1), D)
    grad_rows = jnp.concatenate([out_grad, pad_rows], axis=1).reshape(SEQS * (LEN + 1), D)

    def expert_sums(expert):
        picked = grad_rows[tok_index[expert]].astype(jnp.float32)
        return jnp.dot(picked, w_out[expert].astype(jnp.float32).T)
    sums_all = lax.map(expert_sums, jnp.arange(EXPERTS, dtype=jnp.int32))
    per_route = jnp.zeros((SEQS * (LEN * TOP + 1), HD), jnp.float32)
    per_route = per_route.at[route_index.reshape(-1)].set(sums_all.reshape(-1, HD))
    per_route = per_route.reshape(SEQS, LEN * TOP + 1, HD)[:, :LEN * TOP]
    head_grad = route_gates.reshape(SEQS, LEN * TOP, 1) * per_route

    def per_sequence(operands):
        query_rows, key_rows, value_rows, grad_rows_seq, gate_rows = operands
        return attend(query_rows, key_rows, value_rows, grad_rows_seq, gate_rows, 0)
    query_grad, gated_out, key_sum, value_sum = lax.map(per_sequence, (queries, key_heads, value_heads, head_grad, route_gates))
    pad_heads = jnp.zeros((SEQS, 1, HD), jnp.bfloat16)
    dq_rows = jnp.concatenate([query_grad, pad_heads], axis=1).reshape(SEQS * (LEN * TOP + 1), HD)
    gated_rows = jnp.concatenate([gated_out, pad_heads], axis=1).reshape(SEQS * (LEN * TOP + 1), HD)

    def expert_step(running, expert):
        tok_ids = tok_index[expert]
        rid_ids = route_index[expert]
        hid_part = hid_rows[tok_ids].astype(jnp.float32)
        grad_part = grad_rows[tok_ids].astype(jnp.float32)
        dq_part = dq_rows[rid_ids].astype(jnp.float32)
        gated_part = gated_rows[rid_ids].astype(jnp.float32)
        grad_q_weight = jnp.dot(hid_part.T, dq_part)
        grad_o_weight = jnp.dot(gated_part.T, grad_part)
        route_back = jnp.dot(dq_part, w_query[expert].astype(jnp.float32).T).astype(jnp.bfloat16)
        route_back = lax.optimization_barrier(route_back).astype(jnp.float32)
        running = running.at[tok_ids].add(route_back)
        return (running, (grad_q_weight, grad_o_weight))
    running = jnp.zeros((SEQS * (LEN + 1), D), jnp.float32)
    running, (grad_wq, grad_wo) = lax.scan(expert_step, running, jnp.arange(EXPERTS, dtype=jnp.int32))
    shared_key_gradient = key_sum.astype(jnp.bfloat16).astype(jnp.float32)
    shared_value_gradient = value_sum.astype(jnp.bfloat16).astype(jnp.float32)
    key_matrix = w_key.astype(jnp.float32)
    value_matrix = w_value.astype(jnp.float32)
    grand_total = running.reshape(SEQS, LEN + 1, D)[:, :LEN]
    grand_total = grand_total + jnp.einsum('gwo,zo->gwz', shared_key_gradient, key_matrix) + jnp.einsum('gwo,zo->gwz', shared_value_gradient, value_matrix)
    grad_hidden = grand_total.astype(jnp.bfloat16)
    hidden_single_precision = hidden.astype(jnp.float32)
    key_projection_gradient = jnp.einsum('kfn,kft->nt', hidden_single_precision, shared_key_gradient)
    value_projection_gradient = jnp.einsum('kfn,kft->nt', hidden_single_precision, shared_value_gradient)
    return (grad_hidden, grad_wq, grad_wo, key_projection_gradient, value_projection_gradient)
```

```python
import math

import jax
import jax.numpy as jnp
import numpy as np
from jax import lax
from jax.experimental import pallas as pl
from jax.experimental.pallas import tpu as pltpu
from jax.sharding import Mesh
from jax.sharding import PartitionSpec as P

HD = 128
EXPERTS = 128
TOP = 2
CAP = 3
BLOCK = 128
EPD = 2
ROWS = EPD * CAP
PAD = 8
SEQ = ("x", "zh", "zl")
GRP = ("node", "dev")
SLAB = ("x", "zl")
WIDE = ("x", "zl", "node", "dev")
F32 = jnp.float32
BF16 = jnp.bfloat16
VMEM_LIMIT = 56 * 1024 * 1024


def swap_matrix():
    out = np.arange(8 * 8 * ROWS)
    a, b, q = out // (8 * ROWS), out // ROWS % 8, out % ROWS
    m = np.zeros((8 * 8 * ROWS, 8 * 8 * ROWS), np.float32)
    m[out, b * 8 * ROWS + a * ROWS + q] = 1
    return m


def pad_matrix():
    src = np.arange(8 * 8 * ROWS)
    a, b, q = src // (8 * ROWS), src // ROWS % 8, src % ROWS
    m = np.zeros((8 * 8 * PAD, 8 * 8 * ROWS), np.float32)
    m[b * 8 * PAD + a * PAD + q, src] = 1
    return m


def params(n):
    return pltpu.CompilerParams(dimension_semantics=("arbitrary",) * n, vmem_limit_bytes=VMEM_LIMIT)


def dot_nt(a, b):
    return lax.dot_general(a, b, (((1,), (1,)), ((), ())), preferred_element_type=F32)


def dot_tn(a, b):
    return lax.dot_general(a, b, (((0,), (0,)), ((), ())), preferred_element_type=F32)


def dot_nn(a, b):
    return jnp.dot(a, b, preferred_element_type=F32)


def pack_kernel(routes_ref, hid_ref, grad_ref, swap_ref, hid_out, grad_out, rho_out, stage):
    expert = lax.broadcasted_iota(jnp.int32, (EXPERTS, BLOCK), 0)
    before = (
        lax.broadcasted_iota(jnp.int32, (BLOCK, BLOCK), 0)
        < lax.broadcasted_iota(jnp.int32, (BLOCK, BLOCK), 1)
    ).astype(F32).astype(BF16)
    row_id = lax.broadcasted_iota(jnp.int32, (64 * ROWS, BLOCK), 0)
    for j in range(8):
        x, span = j // 2, pl.ds((j % 2) * BLOCK, BLOCK)
        first = routes_ref[x, 0, 0:1, span]
        second = routes_ref[x, 0, 1:2, span]
        hot_a = (expert == first).astype(F32)
        hot_b = (expert == second).astype(F32)
        earlier = dot_nn((hot_a + hot_b).astype(BF16), before)
        slot_a = jnp.sum(hot_a * earlier, axis=0, keepdims=True).astype(jnp.int32)
        slot_b = jnp.sum(hot_b * earlier, axis=0, keepdims=True).astype(jnp.int32)

        def row_of(e, slot):
            return (((e >> 1) & 7) * 8 + (e >> 4)) * ROWS + (e & 1) * CAP + slot

        rho_a, rho_b = row_of(first, slot_a), row_of(second, slot_b)
        rho_out[x, 0, 0:1, span] = rho_a
        rho_out[x, 0, 1:2, span] = rho_b
        pick = ((row_id == rho_a) | (row_id == rho_b)).astype(F32).astype(BF16)
        both = jnp.concatenate([hid_ref[x, 0, span, :], grad_ref[x, 0, span, :]], axis=1)
        picked = dot_nn(pick, both).astype(BF16)
        for d in range(8):
            stage[d, j * 8 * ROWS : (j + 1) * 8 * ROWS, :] = picked[d * 8 * ROWS : (d + 1) * 8 * ROWS]
    for d in range(8):
        turned = dot_nn(swap_ref[...], stage[d]).astype(BF16).reshape(8, 8 * ROWS, 2 * HD)
        hid_out[d * 8 : (d + 1) * 8, 0] = turned[:, :, :HD]
        grad_out[d * 8 : (d + 1) * 8, 0] = turned[:, :, HD:]


def pack(routes_t, hid, grad, swap):
    slab = pl.BlockSpec((4, 1, 2 * BLOCK, HD), lambda t: (0, t, 0, 0))
    rows = pl.BlockSpec((64, 1, 8 * ROWS, HD), lambda t: (0, t, 0, 0))
    ids = pl.BlockSpec((4, 1, TOP, 2 * BLOCK), lambda t: (0, t, 0, 0))
    return pl.pallas_call(
        pack_kernel,
        grid=(4,),
        in_specs=[ids, slab, slab, pl.BlockSpec(swap.shape, lambda t: (0, 0))],
        out_specs=[rows, rows, ids],
        out_shape=[
            jax.ShapeDtypeStruct((64, 4, 8 * ROWS, HD), BF16),
            jax.ShapeDtypeStruct((64, 4, 8 * ROWS, HD), BF16),
            jax.ShapeDtypeStruct((4, 4, TOP, 2 * BLOCK), jnp.int32),
        ],
        scratch_shapes=[pltpu.VMEM((8, 64 * ROWS, 2 * HD), BF16)],
        compiler_params=params(1),
        name="pack_rows",
    )(routes_t, hid, grad, swap)


def second_expert(shape):
    return lax.rem(lax.broadcasted_iota(jnp.int32, shape, 0), ROWS) >= CAP


def head_kernel(grad_ref, w_ref, out_ref):
    for g in range(2):
        total = dot_nt(grad_ref[0, g], w_ref[0])
        for r in range(1, 8):
            total += dot_nt(grad_ref[r, g], w_ref[r])
        own = jnp.where(second_expert((32 * ROWS, HD)), total[:, HD:], total[:, :HD])
        out_ref[:, g] = own.astype(BF16).reshape(4, 8 * ROWS, HD)


def head_sums(grad_rows, w_out_r):
    return pl.pallas_call(
        head_kernel,
        grid=(4,),
        in_specs=[
            pl.BlockSpec((8, 2, 32 * ROWS, HD), lambda i: (0, i, 0, 0)),
            pl.BlockSpec((8, 2 * HD, HD), lambda i: (0, 0, 0)),
        ],
        out_specs=pl.BlockSpec((4, 2, 8 * ROWS, HD), lambda i: (0, i, 0, 0)),
        out_shape=jax.ShapeDtypeStruct((4, 8, 8 * ROWS, HD), BF16),
        compiler_params=params(1),
        name="head_sums",
    )(grad_rows.reshape(8, 8, 32 * ROWS, HD), w_out_r)


def reduce_kernel(parts_ref, pad_ref, out_ref):
    total = parts_ref[0].astype(F32)
    for s in range(1, 4):
        total += parts_ref[s].astype(F32)
    out_ref[...] = dot_nn(pad_ref[...], total.astype(BF16)).astype(BF16)


def reduce_heads(parts, pad):
    return pl.pallas_call(
        reduce_kernel,
        out_shape=jax.ShapeDtypeStruct((64 * PAD, HD), BF16),
        compiler_params=params(0),
        name="reduce_heads",
    )(parts.reshape(4, 64 * ROWS, HD), pad)


def forward_kernel(start_ref, q_ref, kv_ref, gate_ref, prob_out, head_out, gated_out, score):
    n, length = q_ref.shape[0], kv_ref.shape[0]
    step = 512
    q = q_ref[...]
    pos = start_ref[0] + lax.rem(lax.broadcasted_iota(jnp.int32, (n, step), 0), BLOCK)
    lane = lax.broadcasted_iota(jnp.int32, (n, step), 1)
    top = jnp.full((n, 1), -jnp.inf, F32)
    for c in range(0, length, step):
        s = dot_nt(q, kv_ref[c : c + step, :HD]) * (1.0 / math.sqrt(HD))
        s = jnp.where(lane + c <= pos, s, -jnp.inf)
        score[:, c : c + step] = s
        top = jnp.maximum(top, jnp.max(s, axis=1, keepdims=True))
    total = jnp.zeros((n, 1), F32)
    for c in range(0, length, step):
        w = jnp.exp(score[:, c : c + step] - top)
        score[:, c : c + step] = w
        total += jnp.sum(w, axis=1, keepdims=True)
    inv = 1.0 / total
    out = jnp.zeros((n, HD), F32)
    for c in range(0, length, step):
        p = (score[:, c : c + step] * inv).astype(BF16)
        prob_out[:, c : c + step] = p
        out += dot_nn(p, kv_ref[c : c + step, HD:])
    head_out[...] = out
    gated_out[...] = (gate_ref[...] * out).astype(BF16)


def attend_forward(start, q, kv, gates):
    n, length = q.shape[0], kv.shape[0]
    vm = pl.BlockSpec(memory_space=pltpu.VMEM)
    return pl.pallas_call(
        forward_kernel,
        in_specs=[pl.BlockSpec(memory_space=pltpu.SMEM), vm, vm, vm],
        out_specs=[vm, vm, vm],
        out_shape=[
            jax.ShapeDtypeStruct((n, length), BF16),
            jax.ShapeDtypeStruct((n, HD), F32),
            jax.ShapeDtypeStruct((n, HD), BF16),
        ],
        scratch_shapes=[pltpu.VMEM((n, length), F32)],
        compiler_params=params(0),
        name="attend_forward",
    )(start, q, kv, gates)


def backward_kernel(
    head_ref, rho_row_ref, rho_col_ref, gate_ref, q_ref, kv_ref, prob_ref, out_ref, gated_ref, slots_out, dkv_out
):
    n, length = q_ref.shape[0], kv_ref.shape[0]
    step = 512
    scale = 1.0 / math.sqrt(HD)
    lanes = lax.broadcasted_iota(jnp.int32, (n, 64 * PAD), 1)
    pick = (lanes == rho_col_ref[...]).astype(F32).astype(BF16)
    head_grad = gate_ref[...] * dot_nn(pick, head_ref[...])
    delta = jnp.sum(head_grad * out_ref[...], axis=1, keepdims=True)
    grad = head_grad.astype(BF16)
    q = q_ref[...]
    dq = jnp.zeros((n, HD), F32)
    for c in range(0, length, step):
        keys, values = kv_ref[c : c + step, :HD], kv_ref[c : c + step, HD:]
        p = prob_ref[:, c : c + step]
        ds = (p.astype(F32) * (dot_nt(grad, values) - delta)).astype(BF16)
        dq += dot_nn(ds, keys)
        dkv_out[c : c + step, :HD] = (dot_tn(ds, q) * scale).astype(BF16)
        dkv_out[c : c + step, HD:] = dot_tn(p, grad).astype(BF16)
    both = jnp.concatenate([(dq * scale).astype(BF16), gated_ref[...]], axis=1)
    rows = lax.broadcasted_iota(jnp.int32, (64 * PAD, n), 0)
    place = (rows == rho_row_ref[...]).astype(F32).astype(BF16)
    slots_out[...] = dot_nn(place, both).astype(BF16)


def attend_backward(head, rho_row, rho_col, gates, q, kv, prob, out, gated):
    return pl.pallas_call(
        backward_kernel,
        out_shape=[
            jax.ShapeDtypeStruct((64 * PAD, 2 * HD), BF16),
            jax.ShapeDtypeStruct(kv.shape, BF16),
        ],
        compiler_params=params(0),
        name="attend_backward",
    )(head, rho_row, rho_col, gates, q, kv, prob, out, gated)


def unpad_kernel(rows_ref, unpad_ref, out_ref):
    out_ref[...] = dot_nn(unpad_ref[...], rows_ref[...]).astype(BF16)


def unpad_rows(rows, unpad):
    return pl.pallas_call(
        unpad_kernel,
        out_shape=jax.ShapeDtypeStruct((64 * ROWS, 2 * HD), BF16),
        compiler_params=params(0),
        name="unpad_rows",
    )(rows, unpad)


def by_expert(rows):
    later = second_expert(rows.shape)
    zero = jnp.zeros_like(rows)
    return jnp.concatenate([jnp.where(later, zero, rows), jnp.where(later, rows, zero)], axis=1)


def back_kernel(dqg_ref, w_ref, out_ref):
    for g in range(2):
        dq = by_expert(dqg_ref[:, g, :, :HD].reshape(32 * ROWS, HD))
        for r in range(8):
            out_ref[r, g] = dot_nn(dq, w_ref[r]).astype(BF16)


def route_back(dqg, w_query_r):
    return pl.pallas_call(
        back_kernel,
        grid=(4,),
        in_specs=[
            pl.BlockSpec((4, 2, 8 * ROWS, 2 * HD), lambda i: (0, i, 0, 0)),
            pl.BlockSpec((8, 2 * HD, HD), lambda i: (0, 0, 0)),
        ],
        out_specs=pl.BlockSpec((8, 2, 32 * ROWS, HD), lambda i: (0, i, 0, 0)),
        out_shape=jax.ShapeDtypeStruct((8, 8, 32 * ROWS, HD), BF16),
        compiler_params=params(1),
        name="route_back",
    )(dqg, w_query_r)


def weights_kernel(dqg_ref, hid_ref, grad_ref, wq_out, wo_out, wq_acc, wo_acc):
    @pl.when(pl.program_id(0) == 0)
    def _():
        wq_acc[...] = jnp.zeros_like(wq_acc)
        wo_acc[...] = jnp.zeros_like(wo_acc)

    for g in range(2):
        dq = by_expert(dqg_ref[:, g, :, :HD].reshape(32 * ROWS, HD))
        gated = by_expert(dqg_ref[:, g, :, HD:].reshape(32 * ROWS, HD))
        for r in range(8):
            wq_acc[r] += dot_tn(hid_ref[r, g], dq)
            wo_acc[r] += dot_tn(gated, grad_ref[r, g])

    @pl.when(pl.program_id(0) == 3)
    def _():
        for r in range(8):
            for k in range(EPD):
                wq_out[r, k] = wq_acc[r, :, k * HD : (k + 1) * HD].astype(BF16)
                wo_out[r, k] = wo_acc[r, k * HD : (k + 1) * HD, :].astype(BF16)


def weight_grads(dqg, hid_rows, grad_rows):
    rows = pl.BlockSpec((8, 2, 32 * ROWS, HD), lambda i: (0, i, 0, 0))
    whole = pl.BlockSpec((8, EPD, HD, HD), lambda i: (0, 0, 0, 0))
    return pl.pallas_call(
        weights_kernel,
        grid=(4,),
        in_specs=[pl.BlockSpec((4, 2, 8 * ROWS, 2 * HD), lambda i: (0, i, 0, 0)), rows, rows],
        out_specs=[whole, whole],
        out_shape=[jax.ShapeDtypeStruct((8, EPD, HD, HD), BF16)] * 2,
        scratch_shapes=[pltpu.VMEM((8, HD, EPD * HD), F32), pltpu.VMEM((8, EPD * HD, HD), F32)],
        compiler_params=params(1),
        name="weight_grads",
    )(dqg, hid_rows.reshape(8, 8, 32 * ROWS, HD), grad_rows.reshape(8, 8, 32 * ROWS, HD))


def combine_kernel(rho_ref, back_ref, swap_ref, dkv_ref, wkv_ref, out_ref, stage):
    for d in range(8):
        rows = back_ref[d * 8 : (d + 1) * 8, 0].reshape(64 * ROWS, HD)
        turned = dot_nn(swap_ref[...], rows).astype(BF16)
        for j in range(8):
            stage[j, d * 8 * ROWS : (d + 1) * 8 * ROWS, :] = turned[j * 8 * ROWS : (j + 1) * 8 * ROWS]
    row_id = lax.broadcasted_iota(jnp.int32, (64 * ROWS, BLOCK), 0)
    for j in range(8):
        x, span = j // 2, pl.ds((j % 2) * BLOCK, BLOCK)
        rho_a = rho_ref[x, 0, 0:1, span]
        rho_b = rho_ref[x, 0, 1:2, span]
        pick = ((row_id == rho_a) | (row_id == rho_b)).astype(F32).astype(BF16)
        total = dot_tn(pick, stage[j]) + dot_nt(dkv_ref[x, 0, span, :], wkv_ref[...])
        out_ref[x, 0, span, :] = total.astype(BF16)


def combine(rho, back, swap, dkv, wkv):
    return pl.pallas_call(
        combine_kernel,
        grid=(4,),
        in_specs=[
            pl.BlockSpec((4, 1, TOP, 2 * BLOCK), lambda t: (0, t, 0, 0)),
            pl.BlockSpec((64, 1, 8 * ROWS, HD), lambda t: (0, t, 0, 0)),
            pl.BlockSpec(swap.shape, lambda t: (0, 0)),
            pl.BlockSpec((4, 1, 2 * BLOCK, 2 * HD), lambda t: (0, t, 0, 0)),
            pl.BlockSpec(wkv.shape, lambda t: (0, 0)),
        ],
        out_specs=pl.BlockSpec((4, 1, 2 * BLOCK, HD), lambda t: (0, t, 0, 0)),
        out_shape=jax.ShapeDtypeStruct((4, 4, 2 * BLOCK, HD), BF16),
        scratch_shapes=[pltpu.VMEM((8, 64 * ROWS, HD), BF16)],
        compiler_params=params(1),
        name="combine_rows",
    )(rho, back, swap, dkv, wkv)


def exchange(rows, axes):
    return lax.all_to_all(rows, axes, split_axis=0, concat_axis=0, tiled=True)


def spread(rows, axes):
    n = lax.axis_size(axes)
    return exchange(jnp.broadcast_to(rows[None], (n,) + rows.shape), axes)


def per_device(
    hidden, out_grad, queries, key_heads, value_heads, routes, route_gates, w_query, w_out, w_key, w_value
):
    swap, pad = swap_matrix().astype(BF16), pad_matrix().astype(BF16)
    unpad = pad.T
    xi, zh, zl = lax.axis_index("x"), lax.axis_index("zh"), lax.axis_index("zl")
    kv_own = jnp.concatenate([key_heads[0], value_heads[0]], axis=1)
    kv = lax.all_gather(kv_own, SEQ, axis=0, tiled=True)
    routes_t = routes[0].reshape(4, 4, 2 * BLOCK, TOP).transpose(0, 1, 3, 2)
    hid_packed, grad_packed, rho = pack(
        routes_t,
        hidden[0].reshape(4, 4, 2 * BLOCK, HD),
        out_grad[0].reshape(4, 4, 2 * BLOCK, HD),
        swap,
    )
    grad_rows = exchange(grad_packed, WIDE)
    w_out_r = exchange(w_out, SLAB).reshape(8, EPD * HD, HD)
    w_query_r = exchange(w_query, SLAB).reshape(8, EPD, HD, HD).transpose(0, 1, 3, 2).reshape(8, EPD * HD, HD)
    hid_rows = exchange(hid_packed, WIDE)
    q = queries[0].transpose(1, 0, 2).reshape(TOP * BLOCK, HD)
    gates = route_gates[0].T.reshape(TOP * BLOCK, 1)
    own = lax.dynamic_slice(rho, (xi, zh, 0, zl * BLOCK), (1, 1, TOP, BLOCK)).reshape(TOP * BLOCK)
    own = own // ROWS * PAD + own % ROWS
    start = ((xi * 8 + zh * 2 + zl) * BLOCK).reshape(1)
    prob, head_out, gated = attend_forward(start, q, kv, gates)

    parts = exchange(head_sums(grad_rows, w_out_r), "zh")
    head_home = exchange(reduce_heads(parts, pad).reshape(64, PAD, HD), WIDE)
    slots, dkv_part = attend_backward(
        head_home.reshape(64 * PAD, HD), own.reshape(1, -1), own.reshape(-1, 1), gates, q, kv, prob, head_out, gated
    )
    mine = exchange(slots.reshape(64, PAD, 2 * HD), WIDE).reshape(64 * PAD, 2 * HD)
    dqg = spread(unpad_rows(mine, unpad), "zh").reshape(4, 8, 8 * ROWS, 2 * HD)
    back = exchange(route_back(dqg, w_query_r).reshape(64, 4, 8 * ROWS, HD), WIDE)
    grad_wq, grad_wo = weight_grads(dqg, hid_rows, grad_rows)
    grad_wq = exchange(grad_wq.reshape(16, HD, HD), SLAB).astype(F32)
    grad_wo = exchange(grad_wo.reshape(16, HD, HD), SLAB).astype(F32)

    dkv_x = exchange(dkv_part.reshape(4, 8 * BLOCK, 2 * HD), "x").astype(F32).sum(axis=0).astype(BF16)
    dkv_own = exchange(dkv_x.reshape(8, BLOCK, 2 * HD), ("zh", "zl")).astype(F32).sum(axis=0).astype(BF16)
    dkv = spread(spread(dkv_own, ("zh", "zl")).reshape(8 * BLOCK, 2 * HD), "x")
    dkv = dkv.reshape(4, 4, 2 * BLOCK, 2 * HD)
    wkv = jnp.concatenate([w_key, w_value], axis=1)
    grad_hidden = combine(rho, back, swap, dkv, wkv).reshape(1, 4096, HD)
    proj = lax.dot_general(
        hidden[0], dkv.reshape(-1, 2 * HD), (((0,), (0,)), ((), ())), preferred_element_type=F32
    )
    proj = spread(proj.astype(BF16), GRP).astype(F32).sum(axis=0)
    return (grad_hidden, grad_wq, grad_wo, proj[:, :HD], proj[:, HD:])


def solution(mesh):
    fine = Mesh(mesh.devices.reshape(4, 4, 2, 4, 2), SEQ + GRP)
    in_specs = (
        P(GRP, None, SEQ),
        P(GRP, None, SEQ),
        P(GRP, SEQ, None, None),
        P(GRP, SEQ, None),
        P(GRP, SEQ, None),
        P(GRP, None, None),
        P(GRP, SEQ, None),
        P(GRP, SEQ, None),
        P(GRP, None, SEQ),
        P(SEQ, None),
        P(SEQ, None),
    )
    out_specs = (
        P(GRP, None, SEQ),
        P(GRP, SEQ, None),
        P(GRP, None, SEQ),
        P(SEQ, None),
        P(SEQ, None),
    )
    return jax.shard_map(per_device, mesh=fine, in_specs=in_specs, out_specs=out_specs, check_vma=False)
```

```python
import math

import jax
import jax.numpy as jnp
import numpy as np
from jax import lax
from jax.experimental import pallas as pl
from jax.experimental.pallas import tpu as pltpu
from jax.sharding import Mesh
from jax.sharding import PartitionSpec as P

HD = 128
EXPERTS = 128
TOP = 2
CAP = 3
BLOCK = 128
EPD = 2
ROWS = EPD * CAP
PAD = 8
SEQ = ("x", "zh", "zl")
GRP = ("node", "dev")
SLAB = ("x", "zl")
WIDE = ("x", "zl", "node", "dev")
F32 = jnp.float32
BF16 = jnp.bfloat16
VMEM_LIMIT = 56 * 1024 * 1024


def swap_matrix():
    out = np.arange(8 * 8 * ROWS)
    a, b, q = out // (8 * ROWS), out // ROWS % 8, out % ROWS
    m = np.zeros((8 * 8 * ROWS, 8 * 8 * ROWS), np.float32)
    m[out, b * 8 * ROWS + a * ROWS + q] = 1
    return m


def pad_matrix():
    src = np.arange(8 * 8 * ROWS)
    a, b, q = src // (8 * ROWS), src // ROWS % 8, src % ROWS
    m = np.zeros((8 * 8 * PAD, 8 * 8 * ROWS), np.float32)
    m[b * 8 * PAD + a * PAD + q, src] = 1
    return m


def params(n):
    return pltpu.CompilerParams(dimension_semantics=("arbitrary",) * n, vmem_limit_bytes=VMEM_LIMIT)


def dot_nt(a, b):
    return lax.dot_general(a, b, (((1,), (1,)), ((), ())), preferred_element_type=F32)


def dot_tn(a, b):
    return lax.dot_general(a, b, (((0,), (0,)), ((), ())), preferred_element_type=F32)


def dot_nn(a, b):
    return jnp.dot(a, b, preferred_element_type=F32)


def pack_kernel(routes_ref, hid_ref, grad_ref, swap_ref, hid_out, grad_out, rho_out, stage):
    expert = lax.broadcasted_iota(jnp.int32, (EXPERTS, BLOCK), 0)
    before = (
        lax.broadcasted_iota(jnp.int32, (BLOCK, BLOCK), 0)
        < lax.broadcasted_iota(jnp.int32, (BLOCK, BLOCK), 1)
    ).astype(F32).astype(BF16)
    row_id = lax.broadcasted_iota(jnp.int32, (64 * ROWS, BLOCK), 0)
    for j in range(8):
        x, span = j // 2, pl.ds((j % 2) * BLOCK, BLOCK)
        first = routes_ref[x, 0, 0:1, span]
        second = routes_ref[x, 0, 1:2, span]
        hot_a = (expert == first).astype(F32)
        hot_b = (expert == second).astype(F32)
        earlier = dot_nn((hot_a + hot_b).astype(BF16), before)
        slot_a = jnp.sum(hot_a * earlier, axis=0, keepdims=True).astype(jnp.int32)
        slot_b = jnp.sum(hot_b * earlier, axis=0, keepdims=True).astype(jnp.int32)

        def row_of(e, slot):
            return (((e >> 1) & 7) * 8 + (e >> 4)) * ROWS + (e & 1) * CAP + slot

        rho_a, rho_b = row_of(first, slot_a), row_of(second, slot_b)
        rho_out[x, 0, 0:1, span] = rho_a
        rho_out[x, 0, 1:2, span] = rho_b
        pick = ((row_id == rho_a) | (row_id == rho_b)).astype(F32).astype(BF16)
        both = jnp.concatenate([hid_ref[x, 0, span, :], grad_ref[x, 0, span, :]], axis=1)
        picked = dot_nn(pick, both).astype(BF16)
        for d in range(8):
            stage[d, j * 8 * ROWS : (j + 1) * 8 * ROWS, :] = picked[d * 8 * ROWS : (d + 1) * 8 * ROWS]
    for d in range(8):
        turned = dot_nn(swap_ref[...], stage[d]).astype(BF16).reshape(8, 8 * ROWS, 2 * HD)
        hid_out[d * 8 : (d + 1) * 8, 0] = turned[:, :, :HD]
        grad_out[d * 8 : (d + 1) * 8, 0] = turned[:, :, HD:]


def pack(routes_t, hid, grad, swap):
    slab = pl.BlockSpec((4, 1, 2 * BLOCK, HD), lambda t: (0, t, 0, 0))
    rows = pl.BlockSpec((64, 1, 8 * ROWS, HD), lambda t: (0, t, 0, 0))
    ids = pl.BlockSpec((4, 1, TOP, 2 * BLOCK), lambda t: (0, t, 0, 0))
    return pl.pallas_call(
        pack_kernel,
        grid=(4,),
        in_specs=[ids, slab, slab, pl.BlockSpec(swap.shape, lambda t: (0, 0))],
        out_specs=[rows, rows, ids],
        out_shape=[
            jax.ShapeDtypeStruct((64, 4, 8 * ROWS, HD), BF16),
            jax.ShapeDtypeStruct((64, 4, 8 * ROWS, HD), BF16),
            jax.ShapeDtypeStruct((4, 4, TOP, 2 * BLOCK), jnp.int32),
        ],
        scratch_shapes=[pltpu.VMEM((8, 64 * ROWS, 2 * HD), BF16)],
        cost_estimate=pl.CostEstimate(flops=1000, bytes_accessed=1000, transcendentals=0),
        compiler_params=params(1),
        name="pack_rows",
    )(routes_t, hid, grad, swap)


def second_expert(shape):
    return lax.rem(lax.broadcasted_iota(jnp.int32, shape, 0), ROWS) >= CAP


def head_kernel(at_ref, grad_ref, w_ref, out_ref):
    zh = at_ref[1]
    for g in range(2):
        total = jnp.zeros((32 * ROWS, EPD * HD), F32)
        for r in range(8):
            total += dot_nt(grad_ref[r, g], jnp.concatenate([w_ref[r, 0, 0], w_ref[r, 1, 0]], axis=0))
        own = jnp.where(second_expert((32 * ROWS, HD)), total[:, HD:], total[:, :HD])
        own = own.astype(BF16).reshape(4, 8 * ROWS, HD)
        for t in range(4):
            out_ref[(t + 4 - zh) % 4, g] = own[t]


def head_sums(at, grad_rows, weights):
    return pl.pallas_call(
        head_kernel,
        grid=(4,),
        in_specs=[
            pl.BlockSpec(memory_space=pltpu.SMEM),
            pl.BlockSpec((8, 2, 32 * ROWS, HD), lambda i: (0, i, 0, 0)),
            pl.BlockSpec((8, EPD, 1, HD, HD), lambda i: (0, 0, 0, 0, 0)),
        ],
        out_specs=pl.BlockSpec((4, 2, 8 * ROWS, HD), lambda i: (0, i, 0, 0)),
        out_shape=jax.ShapeDtypeStruct((4, 8, 8 * ROWS, HD), BF16),
        cost_estimate=pl.CostEstimate(flops=1000, bytes_accessed=1000, transcendentals=0),
        compiler_params=params(1),
        name="head_sums",
    )(at, grad_rows.reshape(8, 8, 32 * ROWS, HD), weights)


def reduce_kernel(a_ref, b_ref, c_ref, d_ref, pad_ref, out_ref):
    total = a_ref[...].astype(F32) + b_ref[...].astype(F32) + c_ref[...].astype(F32) + d_ref[...].astype(F32)
    out_ref[...] = dot_nn(pad_ref[...], total.astype(BF16)).astype(BF16)


def reduce_heads(parts, pad):
    return pl.pallas_call(
        reduce_kernel,
        out_shape=jax.ShapeDtypeStruct((64 * PAD, HD), BF16),
        cost_estimate=pl.CostEstimate(flops=1000, bytes_accessed=1000, transcendentals=0),
        compiler_params=params(0),
        name="reduce_heads",
    )(*[p.reshape(64 * ROWS, HD) for p in parts], pad)


def forward_kernel(at_ref, q_ref, kv_ref, gate_ref, prob_out, head_out, gated_out, score):
    n, length = q_ref.shape[0], kv_ref.shape[0]
    step = 512
    q = q_ref[...]
    start = (at_ref[0] * 8 + at_ref[1] * 2 + at_ref[2]) * BLOCK
    pos = start + lax.rem(lax.broadcasted_iota(jnp.int32, (n, step), 0), BLOCK)
    lane = lax.broadcasted_iota(jnp.int32, (n, step), 1)
    top = jnp.full((n, 1), -jnp.inf, F32)
    for c in range(0, length, step):
        s = dot_nt(q, kv_ref[c : c + step, :HD]) * (1.0 / math.sqrt(HD))
        s = jnp.where(lane + c <= pos, s, -jnp.inf)
        score[:, c : c + step] = s
        top = jnp.maximum(top, jnp.max(s, axis=1, keepdims=True))
    total = jnp.zeros((n, 1), F32)
    for c in range(0, length, step):
        w = jnp.exp(score[:, c : c + step] - top)
        score[:, c : c + step] = w
        total += jnp.sum(w, axis=1, keepdims=True)
    inv = 1.0 / total
    out = jnp.zeros((n, HD), F32)
    for c in range(0, length, step):
        p = (score[:, c : c + step] * inv).astype(BF16)
        prob_out[:, c : c + step] = p
        out += dot_nn(p, kv_ref[c : c + step, HD:])
    head_out[...] = out
    gated_out[...] = (gate_ref[...] * out).astype(BF16)


def attend_forward(at, q, kv, gates):
    n, length = q.shape[0], kv.shape[0]
    vm = pl.BlockSpec(memory_space=pltpu.VMEM)
    return pl.pallas_call(
        forward_kernel,
        in_specs=[pl.BlockSpec(memory_space=pltpu.SMEM), vm, vm, vm],
        out_specs=[vm, vm, vm],
        out_shape=[
            jax.ShapeDtypeStruct((n, length), BF16),
            jax.ShapeDtypeStruct((n, HD), F32),
            jax.ShapeDtypeStruct((n, HD), BF16),
        ],
        scratch_shapes=[pltpu.VMEM((n, length), F32)],
        cost_estimate=pl.CostEstimate(flops=1000, bytes_accessed=1000, transcendentals=0),
        compiler_params=params(0),
        name="attend_forward",
    )(at, q, kv, gates)


def backward_kernel(
    head_ref, rho_row_ref, rho_col_ref, gate_ref, q_ref, kv_ref, prob_ref, out_ref, gated_ref, slots_out, dkv_out
):
    n, length = q_ref.shape[0], kv_ref.shape[0]
    step = 512
    scale = 1.0 / math.sqrt(HD)
    lanes = lax.broadcasted_iota(jnp.int32, (n, 64 * PAD), 1)
    pick = (lanes == rho_col_ref[...]).astype(F32).astype(BF16)
    head_grad = gate_ref[...] * dot_nn(pick, head_ref[...])
    delta = jnp.sum(head_grad * out_ref[...], axis=1, keepdims=True)
    grad = head_grad.astype(BF16)
    q = q_ref[...]
    dq = jnp.zeros((n, HD), F32)
    for c in range(0, length, step):
        keys, values = kv_ref[c : c + step, :HD], kv_ref[c : c + step, HD:]
        p = prob_ref[:, c : c + step]
        ds = (p.astype(F32) * (dot_nt(grad, values) - delta)).astype(BF16)
        dq += dot_nn(ds, keys)
        dkv_out[c : c + step, :HD] = (dot_tn(ds, q) * scale).astype(BF16)
        dkv_out[c : c + step, HD:] = dot_tn(p, grad).astype(BF16)
    both = jnp.concatenate([(dq * scale).astype(BF16), gated_ref[...]], axis=1)
    rows = lax.broadcasted_iota(jnp.int32, (64 * PAD, n), 0)
    place = (rows == rho_row_ref[...]).astype(F32).astype(BF16)
    slots_out[...] = dot_nn(place, both).astype(BF16)


def attend_backward(head, rho_row, rho_col, gates, q, kv, prob, out, gated):
    return pl.pallas_call(
        backward_kernel,
        out_shape=[
            jax.ShapeDtypeStruct((64 * PAD, 2 * HD), BF16),
            jax.ShapeDtypeStruct(kv.shape, BF16),
        ],
        cost_estimate=pl.CostEstimate(flops=1000, bytes_accessed=1000, transcendentals=0),
        compiler_params=params(0),
        name="attend_backward",
    )(head, rho_row, rho_col, gates, q, kv, prob, out, gated)


def unpad_kernel(rows_ref, unpad_ref, out_ref):
    out_ref[...] = dot_nn(unpad_ref[...], rows_ref[...]).astype(BF16)


def unpad_rows(rows, unpad):
    return pl.pallas_call(
        unpad_kernel,
        out_shape=jax.ShapeDtypeStruct((64 * ROWS, 2 * HD), BF16),
        cost_estimate=pl.CostEstimate(flops=1000, bytes_accessed=1000, transcendentals=0),
        compiler_params=params(0),
        name="unpad_rows",
    )(rows, unpad)


def by_expert(rows):
    later = second_expert(rows.shape)
    zero = jnp.zeros_like(rows)
    return jnp.concatenate([jnp.where(later, zero, rows), jnp.where(later, rows, zero)], axis=1)


def in_order(at_ref, parts, stage):
    zh = at_ref[1]
    for s, part in enumerate(parts):
        stage[(zh + 4 - s) % 4] = part[...]


def back_kernel(at_ref, a_ref, b_ref, c_ref, d_ref, w_ref, out_ref, dqg_ref):
    in_order(at_ref, (a_ref, b_ref, c_ref, d_ref), dqg_ref)
    for g in range(2):
        dq = by_expert(dqg_ref[:, g, :, :HD].reshape(32 * ROWS, HD))
        for r in range(8):
            w = jnp.concatenate([w_ref[r, 0, 0], w_ref[r, 1, 0]], axis=1)
            out_ref[r, g] = dot_nt(dq, w).astype(BF16)


def route_back(at, dqg, weights):
    return pl.pallas_call(
        back_kernel,
        grid=(4,),
        in_specs=[pl.BlockSpec(memory_space=pltpu.SMEM)]
        + [pl.BlockSpec((2, 8 * ROWS, 2 * HD), lambda i: (i, 0, 0))] * 4
        + [pl.BlockSpec((8, EPD, 1, HD, HD), lambda i: (0, 0, 1, 0, 0))],
        out_specs=pl.BlockSpec((8, 2, 32 * ROWS, HD), lambda i: (0, i, 0, 0)),
        out_shape=jax.ShapeDtypeStruct((8, 8, 32 * ROWS, HD), BF16),
        scratch_shapes=[pltpu.VMEM((4, 2, 8 * ROWS, 2 * HD), BF16)],
        cost_estimate=pl.CostEstimate(flops=1000, bytes_accessed=1000, transcendentals=0),
        compiler_params=params(1),
        name="route_back",
    )(at, *dqg, weights)


def weights_kernel(
    at_ref, a_ref, b_ref, c_ref, d_ref, hid_ref, grad_ref, out_ref, dqg_ref, wq_acc, wo_acc
):
    in_order(at_ref, (a_ref, b_ref, c_ref, d_ref), dqg_ref)

    @pl.when(pl.program_id(0) == 0)
    def _():
        wq_acc[...] = jnp.zeros_like(wq_acc)
        wo_acc[...] = jnp.zeros_like(wo_acc)

    for g in range(2):
        dq = by_expert(dqg_ref[:, g, :, :HD].reshape(32 * ROWS, HD))
        gated = by_expert(dqg_ref[:, g, :, HD:].reshape(32 * ROWS, HD))
        for r in range(8):
            wq_acc[r] += dot_tn(hid_ref[r, g], dq)
            wo_acc[r] += dot_tn(gated, grad_ref[r, g])

    @pl.when(pl.program_id(0) == 3)
    def _():
        for r in range(8):
            for k in range(EPD):
                out_ref[r, k, 0] = wq_acc[r, :, k * HD : (k + 1) * HD].astype(BF16)
                out_ref[r, k, 1] = wo_acc[r, k * HD : (k + 1) * HD, :].astype(BF16)


def weight_grads(at, dqg, hid_rows, grad_rows):
    rows = pl.BlockSpec((8, 2, 32 * ROWS, HD), lambda i: (0, i, 0, 0))
    return pl.pallas_call(
        weights_kernel,
        grid=(4,),
        in_specs=[pl.BlockSpec(memory_space=pltpu.SMEM)]
        + [pl.BlockSpec((2, 8 * ROWS, 2 * HD), lambda i: (i, 0, 0))] * 4
        + [rows, rows],
        out_specs=pl.BlockSpec((8, EPD, 2, HD, HD), lambda i: (0, 0, 0, 0, 0)),
        out_shape=jax.ShapeDtypeStruct((8, EPD, 2, HD, HD), BF16),
        scratch_shapes=[
            pltpu.VMEM((4, 2, 8 * ROWS, 2 * HD), BF16),
            pltpu.VMEM((8, HD, EPD * HD), F32),
            pltpu.VMEM((8, EPD * HD, HD), F32),
        ],
        cost_estimate=pl.CostEstimate(flops=1000, bytes_accessed=1000, transcendentals=0),
        compiler_params=params(1),
        name="weight_grads",
    )(
        at,
        *dqg,
        hid_rows.reshape(8, 8, 32 * ROWS, HD),
        grad_rows.reshape(8, 8, 32 * ROWS, HD),
    )


def projection_kernel(hid_ref, dkv_ref, out_ref):
    out_ref[...] = dot_tn(hid_ref[...], dkv_ref[...]).astype(BF16)


def projection(hid, dkv):
    return pl.pallas_call(
        projection_kernel,
        out_shape=jax.ShapeDtypeStruct((HD, 2 * HD), BF16),
        cost_estimate=pl.CostEstimate(flops=1000, bytes_accessed=1000, transcendentals=0),
        compiler_params=params(0),
        name="projection",
    )(hid, dkv)


def combine_kernel(rho_ref, back_ref, swap_ref, dkv_ref, wkv_ref, out_ref, stage):
    for d in range(8):
        rows = back_ref[d * 8 : (d + 1) * 8, 0].reshape(64 * ROWS, HD)
        turned = dot_nn(swap_ref[...], rows).astype(BF16)
        for j in range(8):
            stage[j, d * 8 * ROWS : (d + 1) * 8 * ROWS, :] = turned[j * 8 * ROWS : (j + 1) * 8 * ROWS]
    row_id = lax.broadcasted_iota(jnp.int32, (64 * ROWS, BLOCK), 0)
    for j in range(8):
        x, span = j // 2, pl.ds((j % 2) * BLOCK, BLOCK)
        rho_a = rho_ref[x, 0, 0:1, span]
        rho_b = rho_ref[x, 0, 1:2, span]
        pick = ((row_id == rho_a) | (row_id == rho_b)).astype(F32).astype(BF16)
        total = dot_tn(pick, stage[j]) + dot_nt(dkv_ref[x, 0, span, :], wkv_ref[...])
        out_ref[x, 0, span, :] = total.astype(BF16)


def combine(rho, back, swap, dkv, wkv):
    return pl.pallas_call(
        combine_kernel,
        grid=(4,),
        in_specs=[
            pl.BlockSpec((4, 1, TOP, 2 * BLOCK), lambda t: (0, t, 0, 0)),
            pl.BlockSpec((64, 1, 8 * ROWS, HD), lambda t: (0, t, 0, 0)),
            pl.BlockSpec(swap.shape, lambda t: (0, 0)),
            pl.BlockSpec((4, 1, 2 * BLOCK, 2 * HD), lambda t: (0, t, 0, 0)),
            pl.BlockSpec(wkv.shape, lambda t: (0, 0)),
        ],
        out_specs=pl.BlockSpec((4, 1, 2 * BLOCK, HD), lambda t: (0, t, 0, 0)),
        out_shape=jax.ShapeDtypeStruct((4, 4, 2 * BLOCK, HD), BF16),
        scratch_shapes=[pltpu.VMEM((8, 64 * ROWS, HD), BF16)],
        cost_estimate=pl.CostEstimate(flops=1000, bytes_accessed=1000, transcendentals=0),
        compiler_params=params(1),
        name="combine_rows",
    )(rho, back, swap, dkv, wkv)


def exchange(rows, axes):
    return lax.all_to_all(rows, axes, split_axis=0, concat_axis=0, tiled=True)


def shifted(rows, axis, s):
    n = lax.axis_size(axis)
    return lax.ppermute(rows, axis, [(i, (i + s) % n) for i in range(n)])


def gather(rows, axis):
    return [rows] + [shifted(rows, axis, s) for s in range(1, lax.axis_size(axis))]


def after(rows, *others):
    return lax.optimization_barrier((rows,) + others)[0]


def per_device(
    hidden, out_grad, queries, key_heads, value_heads, routes, route_gates, w_query, w_out, w_key, w_value
):
    swap, pad = swap_matrix().astype(BF16), pad_matrix().astype(BF16)
    unpad = pad.T
    xi, zh, zl = lax.axis_index("x"), lax.axis_index("zh"), lax.axis_index("zl")
    at = jnp.stack([xi, zh, zl])
    kv = lax.all_gather(jnp.concatenate([key_heads[0], value_heads[0]], axis=1), SEQ, axis=0, tiled=True)
    weights = exchange(jnp.stack([w_out, w_query], axis=1), SLAB).reshape(8, EPD, 2, HD, HD)
    routes_t = routes[0].reshape(4, 4, 2 * BLOCK, TOP).transpose(0, 1, 3, 2)
    hid_packed, grad_packed, rho = pack(
        routes_t,
        hidden[0].reshape(4, 4, 2 * BLOCK, HD),
        out_grad[0].reshape(4, 4, 2 * BLOCK, HD),
        swap,
    )
    grad_rows = exchange(after(grad_packed, weights), WIDE)
    q = queries[0].transpose(1, 0, 2).reshape(TOP * BLOCK, HD)
    gates = route_gates[0].T.reshape(TOP * BLOCK, 1)
    own = lax.dynamic_slice(rho, (xi, zh, 0, zl * BLOCK), (1, 1, TOP, BLOCK)).reshape(TOP * BLOCK)
    own = own // ROWS * PAD + own % ROWS
    prob, head_out, gated = attend_forward(at, q, kv, gates)

    parts = head_sums(at, after(grad_rows, own), weights)
    parts = [parts[0]] + [shifted(parts[s], "zh", s) for s in range(1, 4)]
    head_home = exchange(reduce_heads(parts, pad).reshape(64, PAD, HD), WIDE)
    slots, dkv_part = attend_backward(
        head_home.reshape(64 * PAD, HD), own.reshape(1, -1), own.reshape(-1, 1), gates, q, kv, prob, head_out, gated
    )
    mine = exchange(slots.reshape(64, PAD, 2 * HD), WIDE).reshape(64 * PAD, 2 * HD)
    dkv_x = lax.psum_scatter(dkv_part, "x", scatter_dimension=0, tiled=True)
    dqg = gather(unpad_rows(mine, unpad).reshape(8, 8 * ROWS, 2 * HD), "zh")
    hid_rows = exchange(after(hid_packed, dkv_x, *dqg), WIDE)
    back_rows = route_back(at, dqg, weights).reshape(64, 4, 8 * ROWS, HD)
    dkv_own = lax.psum_scatter(dkv_x, ("zh", "zl"), scatter_dimension=0, tiled=True)
    back = exchange(after(back_rows, hid_rows, dkv_own), WIDE)
    dkv = lax.all_gather(dkv_own, SEQ, axis=0, tiled=True)
    dqg[0] = after(dqg[0], back_rows)
    grads = weight_grads(at, dqg, hid_rows, grad_rows).reshape(16, 2, HD, HD)
    grads = exchange(after(grads, back), SLAB)
    grad_wq, grad_wo = grads[:, 0].astype(F32), grads[:, 1].astype(F32)

    wkv = jnp.concatenate([w_key, w_value], axis=1)
    grad_hidden = combine(rho, back, swap, dkv.reshape(4, 4, 2 * BLOCK, 2 * HD), wkv).reshape(1, 4096, HD)
    proj = projection(hidden[0], dkv)
    proj = sum(p.astype(F32) for p in gather(proj, "dev")).astype(BF16)
    proj = [p.astype(F32) for p in gather(proj, "node")]
    proj = (proj[0] + proj[2]) + (proj[1] + proj[3])
    return (grad_hidden, grad_wq, grad_wo, proj[:, :HD], proj[:, HD:])


def solution(mesh):
    fine = Mesh(mesh.devices.reshape(4, 4, 2, 4, 2), SEQ + GRP)
    in_specs = (
        P(GRP, None, SEQ),
        P(GRP, None, SEQ),
        P(GRP, SEQ, None, None),
        P(GRP, SEQ, None),
        P(GRP, SEQ, None),
        P(GRP, None, None),
        P(GRP, SEQ, None),
        P(GRP, SEQ, None),
        P(GRP, None, SEQ),
        P(SEQ, None),
        P(SEQ, None),
    )
    out_specs = (
        P(GRP, None, SEQ),
        P(GRP, SEQ, None),
        P(GRP, None, SEQ),
        P(SEQ, None),
        P(SEQ, None),
    )
    return jax.shard_map(per_device, mesh=fine, in_specs=in_specs, out_specs=out_specs, check_vma=False)
```

```python
import math

import jax
import jax.numpy as jnp
import numpy as np
from jax import lax
from jax.experimental import pallas as pl
from jax.experimental.pallas import tpu as pltpu
from jax.sharding import Mesh
from jax.sharding import PartitionSpec as P

HD = 128
EXPERTS = 128
TOP = 2
CAP = 3
BLOCK = 128
EPD = 2
ROWS = EPD * CAP
PAD = 8
SEQ = ("x", "zh", "zl")
GRP = ("node", "dev")
SLAB = ("x", "zl")
WIDE = ("x", "zl", "node", "dev")
F32 = jnp.float32
BF16 = jnp.bfloat16
VMEM_LIMIT = 56 * 1024 * 1024


def swap_matrix():
    out = np.arange(8 * 8 * ROWS)
    a, b, q = out // (8 * ROWS), out // ROWS % 8, out % ROWS
    m = np.zeros((8 * 8 * ROWS, 8 * 8 * ROWS), np.float32)
    m[out, b * 8 * ROWS + a * ROWS + q] = 1
    return m


def pad_matrix():
    src = np.arange(8 * 8 * ROWS)
    a, b, q = src // (8 * ROWS), src // ROWS % 8, src % ROWS
    m = np.zeros((8 * 8 * PAD, 8 * 8 * ROWS), np.float32)
    m[b * 8 * PAD + a * PAD + q, src] = 1
    return m


def params(n):
    return pltpu.CompilerParams(dimension_semantics=("arbitrary",) * n, vmem_limit_bytes=VMEM_LIMIT)


def dot_nt(a, b):
    return lax.dot_general(a, b, (((1,), (1,)), ((), ())), preferred_element_type=F32)


def dot_tn(a, b):
    return lax.dot_general(a, b, (((0,), (0,)), ((), ())), preferred_element_type=F32)


def dot_nn(a, b):
    return jnp.dot(a, b, preferred_element_type=F32)


def pack_rows(refs, rho_of, swap_ref, out_ref, stage):
    row_id = lax.broadcasted_iota(jnp.int32, (64 * ROWS, BLOCK), 0)
    for j in range(8):
        x, span = j // 2, pl.ds((j % 2) * BLOCK, BLOCK)
        rho_a, rho_b = rho_of(x, span)
        pick = ((row_id == rho_a) | (row_id == rho_b)).astype(F32).astype(BF16)
        picked = dot_nn(pick, refs[x, 0, span, :]).astype(BF16)
        for d in range(8):
            stage[d, j * 8 * ROWS : (j + 1) * 8 * ROWS, :] = picked[d * 8 * ROWS : (d + 1) * 8 * ROWS]
    for d in range(8):
        turned = dot_nn(swap_ref[...], stage[d]).astype(BF16)
        out_ref[d * 8 : (d + 1) * 8, 0] = turned.reshape(8, 8 * ROWS, HD)


def pack_first_kernel(routes_ref, rows_ref, swap_ref, packed_out, rho_out, stage):
    expert = lax.broadcasted_iota(jnp.int32, (EXPERTS, BLOCK), 0)
    before = (
        lax.broadcasted_iota(jnp.int32, (BLOCK, BLOCK), 0)
        < lax.broadcasted_iota(jnp.int32, (BLOCK, BLOCK), 1)
    ).astype(F32).astype(BF16)

    def row_of(e, slot):
        return (((e >> 1) & 7) * 8 + (e >> 4)) * ROWS + (e & 1) * CAP + slot

    def rho_of(x, span):
        first = routes_ref[x, 0, 0:1, span]
        second = routes_ref[x, 0, 1:2, span]
        hot_a = (expert == first).astype(F32)
        hot_b = (expert == second).astype(F32)
        earlier = dot_nn((hot_a + hot_b).astype(BF16), before)
        rho_a = row_of(first, jnp.sum(hot_a * earlier, axis=0, keepdims=True).astype(jnp.int32))
        rho_b = row_of(second, jnp.sum(hot_b * earlier, axis=0, keepdims=True).astype(jnp.int32))
        rho_out[x, 0, 0:1, span] = rho_a
        rho_out[x, 0, 1:2, span] = rho_b
        return rho_a, rho_b

    pack_rows(rows_ref, rho_of, swap_ref, packed_out, stage)


def pack_again_kernel(rho_ref, rows_ref, swap_ref, packed_out, stage):
    def rho_of(x, span):
        return rho_ref[x, 0, 0:1, span], rho_ref[x, 0, 1:2, span]

    pack_rows(rows_ref, rho_of, swap_ref, packed_out, stage)


def pack(kernel, ids, rows, swap, with_rho, first, steps):
    slab = pl.BlockSpec((4, 1, 2 * BLOCK, HD), lambda t: (0, t + first, 0, 0))
    packed = pl.BlockSpec((64, 1, 8 * ROWS, HD), lambda t: (0, t, 0, 0))
    id_spec = pl.BlockSpec((4, 1, TOP, 2 * BLOCK), lambda t: (0, t + first, 0, 0))
    shapes = [
        jax.ShapeDtypeStruct((64, steps, 8 * ROWS, HD), BF16),
        jax.ShapeDtypeStruct((4, 4, TOP, 2 * BLOCK), jnp.int32),
    ]
    return pl.pallas_call(
        kernel,
        grid=(steps,),
        in_specs=[id_spec, slab, pl.BlockSpec(swap.shape, lambda t: (0, 0))],
        out_specs=[packed, id_spec][: 1 + with_rho],
        out_shape=shapes[: 1 + with_rho],
        scratch_shapes=[pltpu.VMEM((8, 64 * ROWS, HD), BF16)],
        cost_estimate=pl.CostEstimate(flops=1000, bytes_accessed=1000, transcendentals=0),
        compiler_params=params(1),
        name="pack_rows",
    )(ids, rows, swap)


def second_expert(shape):
    return lax.rem(lax.broadcasted_iota(jnp.int32, shape, 0), ROWS) >= CAP


def head_kernel(at_ref, grad_ref, w_ref, out_ref):
    zh = at_ref[1]
    for g in range(2):
        total = jnp.zeros((32 * ROWS, EPD * HD), F32)
        for r in range(8):
            total += dot_nt(grad_ref[r, g], w_ref[r])
        own = jnp.where(second_expert((32 * ROWS, HD)), total[:, HD:], total[:, :HD])
        own = own.astype(BF16).reshape(4, 8 * ROWS, HD)
        for t in range(4):
            out_ref[(t + 4 - zh) % 4, g] = own[t]


def head_sums(at, grad_rows, weights):
    return pl.pallas_call(
        head_kernel,
        grid=(4,),
        in_specs=[
            pl.BlockSpec(memory_space=pltpu.SMEM),
            pl.BlockSpec((8, 2, 32 * ROWS, HD), lambda i: (0, i, 0, 0)),
            pl.BlockSpec((8, EPD * HD, HD), lambda i: (0, 0, 0)),
        ],
        out_specs=pl.BlockSpec((4, 2, 8 * ROWS, HD), lambda i: (0, i, 0, 0)),
        out_shape=jax.ShapeDtypeStruct((4, 8, 8 * ROWS, HD), BF16),
        cost_estimate=pl.CostEstimate(flops=1000, bytes_accessed=1000, transcendentals=0),
        compiler_params=params(1),
        name="head_sums",
    )(at, grad_rows.reshape(8, 8, 32 * ROWS, HD), weights)


def reduce_kernel(a_ref, b_ref, c_ref, d_ref, pad_ref, out_ref):
    total = a_ref[...].astype(F32) + b_ref[...].astype(F32) + c_ref[...].astype(F32) + d_ref[...].astype(F32)
    out_ref[...] = dot_nn(pad_ref[...], total.astype(BF16)).astype(BF16)


def reduce_heads(parts, pad):
    return pl.pallas_call(
        reduce_kernel,
        out_shape=jax.ShapeDtypeStruct((64 * PAD, HD), BF16),
        cost_estimate=pl.CostEstimate(flops=1000, bytes_accessed=1000, transcendentals=0),
        compiler_params=params(0),
        name="reduce_heads",
    )(*[p.reshape(64 * ROWS, HD) for p in parts], pad)


def forward_kernel(at_ref, q_ref, kv_ref, gate_ref, prob_out, head_out, gated_out, score):
    n, length = q_ref.shape[0], kv_ref.shape[0]
    step = 512
    q = q_ref[...]
    start = (at_ref[0] * 8 + at_ref[1] * 2 + at_ref[2]) * BLOCK
    pos = start + lax.rem(lax.broadcasted_iota(jnp.int32, (n, step), 0), BLOCK)
    lane = lax.broadcasted_iota(jnp.int32, (n, step), 1)
    top = jnp.full((n, 1), -jnp.inf, F32)
    for c in range(0, length, step):
        s = dot_nt(q, kv_ref[c : c + step, :HD]) * (1.0 / math.sqrt(HD))
        s = jnp.where(lane + c <= pos, s, -jnp.inf)
        score[:, c : c + step] = s
        top = jnp.maximum(top, jnp.max(s, axis=1, keepdims=True))
    total = jnp.zeros((n, 1), F32)
    for c in range(0, length, step):
        w = jnp.exp(score[:, c : c + step] - top)
        score[:, c : c + step] = w
        total += jnp.sum(w, axis=1, keepdims=True)
    inv = 1.0 / total
    out = jnp.zeros((n, HD), F32)
    for c in range(0, length, step):
        p = (score[:, c : c + step] * inv).astype(BF16)
        prob_out[:, c : c + step] = p
        out += dot_nn(p, kv_ref[c : c + step, HD:])
    head_out[...] = out
    gated_out[...] = (gate_ref[...] * out).astype(BF16)


def attend_forward(at, q, kv, gates):
    n, length = q.shape[0], kv.shape[0]
    vm = pl.BlockSpec(memory_space=pltpu.VMEM)
    return pl.pallas_call(
        forward_kernel,
        in_specs=[pl.BlockSpec(memory_space=pltpu.SMEM), vm, vm, vm],
        out_specs=[vm, vm, vm],
        out_shape=[
            jax.ShapeDtypeStruct((n, length), BF16),
            jax.ShapeDtypeStruct((n, HD), F32),
            jax.ShapeDtypeStruct((n, HD), BF16),
        ],
        scratch_shapes=[pltpu.VMEM((n, length), F32)],
        cost_estimate=pl.CostEstimate(flops=1000, bytes_accessed=1000, transcendentals=0),
        compiler_params=params(0),
        name="attend_forward",
    )(at, q, kv, gates)


def backward_kernel(
    head_ref, rho_row_ref, rho_col_ref, gate_ref, q_ref, kv_ref, prob_ref, out_ref, gated_ref, slots_out, dkv_out
):
    n, length = q_ref.shape[0], kv_ref.shape[0]
    step = 512
    scale = 1.0 / math.sqrt(HD)
    lanes = lax.broadcasted_iota(jnp.int32, (n, 64 * PAD), 1)
    pick = (lanes == rho_col_ref[...]).astype(F32).astype(BF16)
    head_grad = gate_ref[...] * dot_nn(pick, head_ref[...])
    delta = jnp.sum(head_grad * out_ref[...], axis=1, keepdims=True)
    grad = head_grad.astype(BF16)
    q = q_ref[...]
    dq = jnp.zeros((n, HD), F32)
    for c in range(0, length, step):
        keys, values = kv_ref[c : c + step, :HD], kv_ref[c : c + step, HD:]
        p = prob_ref[:, c : c + step]
        ds = (p.astype(F32) * (dot_nt(grad, values) - delta)).astype(BF16)
        dq += dot_nn(ds, keys)
        dkv_out[c : c + step, :HD] = (dot_tn(ds, q) * scale).astype(BF16)
        dkv_out[c : c + step, HD:] = dot_tn(p, grad).astype(BF16)
    both = jnp.concatenate([(dq * scale).astype(BF16), gated_ref[...]], axis=1)
    rows = lax.broadcasted_iota(jnp.int32, (64 * PAD, n), 0)
    place = (rows == rho_row_ref[...]).astype(F32).astype(BF16)
    slots_out[...] = dot_nn(place, both).astype(BF16)


def attend_backward(head, rho_row, rho_col, gates, q, kv, prob, out, gated):
    return pl.pallas_call(
        backward_kernel,
        out_shape=[
            jax.ShapeDtypeStruct((64 * PAD, 2 * HD), BF16),
            jax.ShapeDtypeStruct(kv.shape, BF16),
        ],
        cost_estimate=pl.CostEstimate(flops=1000, bytes_accessed=1000, transcendentals=0),
        compiler_params=params(0),
        name="attend_backward",
    )(head, rho_row, rho_col, gates, q, kv, prob, out, gated)


def unpad_kernel(rows_ref, unpad_ref, out_ref):
    out_ref[...] = dot_nn(unpad_ref[...], rows_ref[...]).astype(BF16)


def unpad_rows(rows, unpad):
    return pl.pallas_call(
        unpad_kernel,
        out_shape=jax.ShapeDtypeStruct((64 * ROWS, 2 * HD), BF16),
        cost_estimate=pl.CostEstimate(flops=10000000000, bytes_accessed=4000000, transcendentals=0),
        compiler_params=params(0),
        name="unpad_rows",
    )(rows, unpad)


def by_expert(rows):
    later = second_expert(rows.shape)
    zero = jnp.zeros_like(rows)
    return jnp.concatenate([jnp.where(later, zero, rows), jnp.where(later, rows, zero)], axis=1)


def in_order(at_ref, parts, stage):
    zh = at_ref[1]
    for s, part in enumerate(parts):
        stage[(zh + 4 - s) % 4] = part[...]


def back_kernel(at_ref, a_ref, b_ref, c_ref, d_ref, w_ref, out_ref, dqg_ref):
    in_order(at_ref, (a_ref, b_ref, c_ref, d_ref), dqg_ref)
    for g in range(2):
        dq = by_expert(dqg_ref[:, g, :, :HD].reshape(32 * ROWS, HD))
        for r in range(8):
            w = jnp.concatenate([w_ref[r, 0], w_ref[r, 1]], axis=1)
            out_ref[r, g] = dot_nt(dq, w).astype(BF16)


def route_back(at, dqg, weights):
    return pl.pallas_call(
        back_kernel,
        grid=(4,),
        in_specs=[pl.BlockSpec(memory_space=pltpu.SMEM)]
        + [pl.BlockSpec((2, 8 * ROWS, 2 * HD), lambda i: (i, 0, 0))] * 4
        + [pl.BlockSpec((8, EPD, HD, HD), lambda i: (0, 0, 0, 0))],
        out_specs=pl.BlockSpec((8, 2, 32 * ROWS, HD), lambda i: (0, i, 0, 0)),
        out_shape=jax.ShapeDtypeStruct((8, 8, 32 * ROWS, HD), BF16),
        scratch_shapes=[pltpu.VMEM((4, 2, 8 * ROWS, 2 * HD), BF16)],
        cost_estimate=pl.CostEstimate(flops=1000, bytes_accessed=1000, transcendentals=0),
        compiler_params=params(1),
        name="route_back",
    )(at, *dqg, weights)


def early_weights_kernel(at_ref, a_ref, b_ref, c_ref, d_ref, hid_ref, grad_ref, wq_acc, wo_acc, dqg_ref):
    in_order(at_ref, (a_ref, b_ref, c_ref, d_ref), dqg_ref)

    @pl.when(pl.program_id(0) == 0)
    def _():
        wq_acc[...] = jnp.zeros_like(wq_acc)
        wo_acc[...] = jnp.zeros_like(wo_acc)

    for g in range(2):
        dq = by_expert(dqg_ref[:2, g, :, :HD].reshape(16 * ROWS, HD))
        gated = by_expert(dqg_ref[:, g, :, HD:].reshape(32 * ROWS, HD))
        for r in range(8):
            wq_acc[r] += dot_tn(hid_ref[r, g], dq)
            wo_acc[r] += dot_tn(gated, grad_ref[r, g])


def late_weights_kernel(at_ref, a_ref, b_ref, c_ref, d_ref, hid_ref, wq_ref, wo_ref, out_ref, dqg_ref, wq_acc):
    in_order(at_ref, (a_ref, b_ref, c_ref, d_ref), dqg_ref)

    @pl.when(pl.program_id(0) == 0)
    def _():
        wq_acc[...] = wq_ref[...]
        for r in range(8):
            for k in range(EPD):
                out_ref[r, k, 1] = wo_ref[r, k * HD : (k + 1) * HD, :].astype(BF16)

    for g in range(2):
        dq = by_expert(dqg_ref[2:, g, :, :HD].reshape(16 * ROWS, HD))
        for r in range(8):
            wq_acc[r] += dot_tn(hid_ref[r, g], dq)

    @pl.when(pl.program_id(0) == 3)
    def _():
        for r in range(8):
            for k in range(EPD):
                out_ref[r, k, 0] = wq_acc[r, :, k * HD : (k + 1) * HD].astype(BF16)


def weights_call(kernel, name, operands, in_specs, out_shapes, scratch):
    def whole(shape):
        return pl.BlockSpec(shape, lambda i: (0,) * len(shape))

    return pl.pallas_call(
        kernel,
        grid=(4,),
        in_specs=[pl.BlockSpec(memory_space=pltpu.SMEM)]
        + [pl.BlockSpec((2, 8 * ROWS, 2 * HD), lambda i: (i, 0, 0))] * 4
        + in_specs
        + [whole(o.shape) for o in operands[5 + len(in_specs) :]],
        out_specs=[whole(o.shape) for o in out_shapes],
        out_shape=out_shapes,
        scratch_shapes=[pltpu.VMEM((4, 2, 8 * ROWS, 2 * HD), BF16)] + scratch,
        cost_estimate=pl.CostEstimate(flops=1000, bytes_accessed=1000, transcendentals=0),
        compiler_params=params(1),
        name=name,
    )(*operands)


def early_weights(at, dqg, hid_a, grad_rows):
    return weights_call(
        early_weights_kernel,
        "early_weights",
        [at, *dqg, hid_a.reshape(8, 8, 16 * ROWS, HD), grad_rows.reshape(8, 8, 32 * ROWS, HD)],
        [
            pl.BlockSpec((8, 2, 16 * ROWS, HD), lambda i: (0, i, 0, 0)),
            pl.BlockSpec((8, 2, 32 * ROWS, HD), lambda i: (0, i, 0, 0)),
        ],
        [
            jax.ShapeDtypeStruct((8, HD, EPD * HD), F32),
            jax.ShapeDtypeStruct((8, EPD * HD, HD), F32),
        ],
        [],
    )


def late_weights(at, dqg, hid_b, wq, wo):
    (out,) = weights_call(
        late_weights_kernel,
        "late_weights",
        [at, *dqg, hid_b.reshape(8, 8, 16 * ROWS, HD), wq, wo],
        [pl.BlockSpec((8, 2, 16 * ROWS, HD), lambda i: (0, i, 0, 0))],
        [jax.ShapeDtypeStruct((8, EPD, 2, HD, HD), BF16)],
        [pltpu.VMEM((8, HD, EPD * HD), F32)],
    )
    return out


def projection_kernel(hid_ref, dkv_ref, out_ref):
    out_ref[...] = dot_tn(hid_ref[...], dkv_ref[...]).astype(BF16)


def projection(hid, dkv):
    return pl.pallas_call(
        projection_kernel,
        out_shape=jax.ShapeDtypeStruct((HD, 2 * HD), BF16),
        cost_estimate=pl.CostEstimate(flops=1000, bytes_accessed=1000, transcendentals=0),
        compiler_params=params(0),
        name="projection",
    )(hid, dkv)


def unpack_kernel(rho_ref, back_ref, swap_ref, out_ref, stage):
    for d in range(8):
        rows = back_ref[d * 8 : (d + 1) * 8, 0].reshape(64 * ROWS, HD)
        turned = dot_nn(swap_ref[...], rows).astype(BF16)
        for j in range(8):
            stage[j, d * 8 * ROWS : (d + 1) * 8 * ROWS, :] = turned[j * 8 * ROWS : (j + 1) * 8 * ROWS]
    row_id = lax.broadcasted_iota(jnp.int32, (64 * ROWS, BLOCK), 0)
    for j in range(8):
        x, span = j // 2, pl.ds((j % 2) * BLOCK, BLOCK)
        rho_a = rho_ref[x, 0, 0:1, span]
        rho_b = rho_ref[x, 0, 1:2, span]
        pick = ((row_id == rho_a) | (row_id == rho_b)).astype(F32).astype(BF16)
        out_ref[x, 0, span, :] = dot_tn(pick, stage[j])


def unpack(rho, back, swap):
    return pl.pallas_call(
        unpack_kernel,
        grid=(4,),
        in_specs=[
            pl.BlockSpec((4, 1, TOP, 2 * BLOCK), lambda t: (0, t, 0, 0)),
            pl.BlockSpec((64, 1, 8 * ROWS, HD), lambda t: (0, t, 0, 0)),
            pl.BlockSpec(swap.shape, lambda t: (0, 0)),
        ],
        out_specs=pl.BlockSpec((4, 1, 2 * BLOCK, HD), lambda t: (0, t, 0, 0)),
        out_shape=jax.ShapeDtypeStruct((4, 4, 2 * BLOCK, HD), F32),
        scratch_shapes=[pltpu.VMEM((8, 64 * ROWS, HD), BF16)],
        cost_estimate=pl.CostEstimate(flops=1000, bytes_accessed=1000, transcendentals=0),
        compiler_params=params(1),
        name="unpack_rows",
    )(rho, back, swap)


def finish_kernel(rows_ref, dkv_ref, wkv_ref, out_ref):
    for x in range(4):
        total = rows_ref[x, 0] + dot_nt(dkv_ref[x, 0], wkv_ref[...])
        out_ref[x, 0] = total.astype(BF16)


def finish(rows, dkv, wkv):
    return pl.pallas_call(
        finish_kernel,
        grid=(4,),
        in_specs=[
            pl.BlockSpec((4, 1, 2 * BLOCK, HD), lambda t: (0, t, 0, 0)),
            pl.BlockSpec((4, 1, 2 * BLOCK, 2 * HD), lambda t: (0, t, 0, 0)),
            pl.BlockSpec(wkv.shape, lambda t: (0, 0)),
        ],
        out_specs=pl.BlockSpec((4, 1, 2 * BLOCK, HD), lambda t: (0, t, 0, 0)),
        out_shape=jax.ShapeDtypeStruct((4, 4, 2 * BLOCK, HD), BF16),
        cost_estimate=pl.CostEstimate(flops=5000000000, bytes_accessed=10000000, transcendentals=0),
        compiler_params=params(1),
        name="finish_rows",
    )(rows, dkv, wkv)


def exchange(rows, axes):
    return lax.all_to_all(rows, axes, split_axis=0, concat_axis=0, tiled=True)


def shifted(rows, axis, s):
    n = lax.axis_size(axis)
    return lax.ppermute(rows, axis, [(i, (i + s) % n) for i in range(n)])


def gather(rows, axis):
    return [rows] + [shifted(rows, axis, s) for s in range(1, lax.axis_size(axis))]


def after(rows, *others):
    return lax.optimization_barrier((rows,) + others)[0]


def per_device(
    hidden, out_grad, queries, key_heads, value_heads, routes, route_gates, w_query, w_out, w_key, w_value
):
    swap, pad = swap_matrix().astype(BF16), pad_matrix().astype(BF16)
    unpad = pad.T
    xi, zh, zl = lax.axis_index("x"), lax.axis_index("zh"), lax.axis_index("zl")
    at = jnp.stack([xi, zh, zl])
    kv = lax.all_gather(jnp.concatenate([key_heads[0], value_heads[0]], axis=1), SEQ, axis=0, tiled=True)
    routes_t = routes[0].reshape(4, 4, 2 * BLOCK, TOP).transpose(0, 1, 3, 2)
    slab = (4, 4, 2 * BLOCK, HD)
    grad_packed, rho = pack(pack_first_kernel, routes_t, out_grad[0].reshape(slab), swap, 1, 0, 4)
    w_out_r = exchange(w_out, SLAB).reshape(8, EPD * HD, HD)
    grad_rows = exchange(after(grad_packed, w_out_r), WIDE)
    (hid_a,) = pack(pack_again_kernel, rho, hidden[0].reshape(slab), swap, 0, 0, 2)
    (hid_b,) = pack(pack_again_kernel, rho, hidden[0].reshape(slab), swap, 0, 2, 2)
    q = queries[0].transpose(1, 0, 2).reshape(TOP * BLOCK, HD)
    gates = route_gates[0].T.reshape(TOP * BLOCK, 1)
    own = lax.dynamic_slice(rho, (xi, zh, 0, zl * BLOCK), (1, 1, TOP, BLOCK)).reshape(TOP * BLOCK)
    own = own // ROWS * PAD + own % ROWS
    own_row, own_col = own.reshape(1, -1), own.reshape(-1, 1)

    parts = head_sums(at, after(grad_rows, own_row, own_col, q, gates, hid_a, hid_b), w_out_r)
    w_query_r = exchange(after(w_query, grad_rows, own_row, own_col, q, gates, hid_a, hid_b), SLAB).reshape(8, EPD, HD, HD)
    parts = list(lax.optimization_barrier((*[parts[s] for s in range(4)], w_query_r)))[:4]
    parts = [parts[0]] + [shifted(parts[s], "zh", s) for s in range(1, 4)]
    head_home = exchange(reduce_heads(parts, pad).reshape(64, PAD, HD), WIDE)
    hid_a = exchange(after(hid_a, head_home), WIDE)
    prob, head_out, gated = attend_forward(at, after(q, head_home), kv, gates)
    slots, dkv_part = attend_backward(
        head_home.reshape(64 * PAD, HD), own_row, own_col, gates, q, kv,
        prob, head_out, gated,
    )
    dkv_x = lax.psum_scatter(dkv_part, "x", scatter_dimension=0, tiled=True)
    mine = exchange(after(slots, hid_a).reshape(64, PAD, 2 * HD), WIDE).reshape(64 * PAD, 2 * HD)
    dqg = unpad_rows(mine, unpad).reshape(8, 8 * ROWS, 2 * HD)
    dqg = gather(dqg, "zh")
    dkv_z = exchange(after(dkv_x, *dqg).reshape(8, BLOCK, 2 * HD), ("zh", "zl"))
    dkv_own = dkv_z.astype(F32).sum(axis=0).astype(BF16)
    dkv = lax.all_gather(dkv_own, SEQ, axis=0, tiled=True)
    back_rows = route_back(at, dqg, w_query_r).reshape(64, 4, 8 * ROWS, HD)
    back = exchange(after(back_rows, dkv_z), WIDE)
    hid_b = exchange(after(hid_b, back), WIDE)
    unpacked = unpack(rho, back, swap)
    dqg[0] = after(dqg[0], back_rows)
    wq, wo = early_weights(at, dqg, hid_a, grad_rows)
    dqg[0] = after(dqg[0], unpacked, wq)
    grads = late_weights(at, dqg, hid_b, wq, wo).reshape(16, 2, HD, HD)
    grads = exchange(grads, SLAB)
    grad_wq, grad_wo = grads[:, 0].astype(F32), grads[:, 1].astype(F32)

    wkv = jnp.concatenate([w_key, w_value], axis=1)
    proj = projection(hidden[0], dkv)
    grad_hidden = finish(unpacked, dkv.reshape(4, 4, 2 * BLOCK, 2 * HD), wkv).reshape(1, 4096, HD)
    proj = sum(p.astype(F32) for p in gather(proj, "dev")).astype(BF16)
    proj = [p.astype(F32) for p in gather(proj, "node")]
    proj[0] = after(proj[0], grad_hidden)
    proj = (proj[0] + proj[2]) + (proj[1] + proj[3])
    return (grad_hidden, grad_wq, grad_wo, proj[:, :HD], proj[:, HD:])


def solution(mesh):
    fine = Mesh(mesh.devices.reshape(4, 4, 2, 4, 2), SEQ + GRP)
    in_specs = (
        P(GRP, None, SEQ),
        P(GRP, None, SEQ),
        P(GRP, SEQ, None, None),
        P(GRP, SEQ, None),
        P(GRP, SEQ, None),
        P(GRP, None, None),
        P(GRP, SEQ, None),
        P(GRP, SEQ, None),
        P(GRP, None, SEQ),
        P(SEQ, None),
        P(SEQ, None),
    )
    out_specs = (
        P(GRP, None, SEQ),
        P(GRP, SEQ, None),
        P(GRP, None, SEQ),
        P(SEQ, None),
        P(SEQ, None),
    )
    return jax.shard_map(per_device, mesh=fine, in_specs=in_specs, out_specs=out_specs, check_vma=False)
```

```python
import math

import jax
import jax.numpy as jnp
import numpy as np
from jax import lax
from jax.experimental import pallas as pl
from jax.experimental.pallas import tpu as pltpu
from jax.sharding import Mesh
from jax.sharding import PartitionSpec as P

HD = 128
EXPERTS = 128
TOP = 2
CAP = 3
BLOCK = 128
EPD = 2
ROWS = EPD * CAP
PAD = 8
SEQ = ("x", "zh", "zl")
GRP = ("node", "dev")
SLAB = ("x", "zl")
WIDE = ("x", "zl", "node", "dev")
F32 = jnp.float32
BF16 = jnp.bfloat16
VMEM_LIMIT = 56 * 1024 * 1024


def swap_matrix():
    out = np.arange(8 * 8 * ROWS)
    a, b, q = out // (8 * ROWS), out // ROWS % 8, out % ROWS
    m = np.zeros((8 * 8 * ROWS, 8 * 8 * ROWS), np.float32)
    m[out, b * 8 * ROWS + a * ROWS + q] = 1
    return m


def pad_matrix():
    src = np.arange(8 * 8 * ROWS)
    a, b, q = src // (8 * ROWS), src // ROWS % 8, src % ROWS
    m = np.zeros((8 * 8 * PAD, 8 * 8 * ROWS), np.float32)
    m[b * 8 * PAD + a * PAD + q, src] = 1
    return m


def params(n):
    return pltpu.CompilerParams(dimension_semantics=("arbitrary",) * n, vmem_limit_bytes=VMEM_LIMIT)


def dot_nt(a, b):
    return lax.dot_general(a, b, (((1,), (1,)), ((), ())), preferred_element_type=F32)


def dot_tn(a, b):
    return lax.dot_general(a, b, (((0,), (0,)), ((), ())), preferred_element_type=F32)


def dot_nn(a, b):
    return jnp.dot(a, b, preferred_element_type=F32)


def pack_rows(refs, rho_of, swap_ref, out_ref, stage):
    row_id = lax.broadcasted_iota(jnp.int32, (64 * ROWS, BLOCK), 0)
    for j in range(8):
        x, span = j // 2, pl.ds((j % 2) * BLOCK, BLOCK)
        rho_a, rho_b = rho_of(x, span)
        pick = ((row_id == rho_a) | (row_id == rho_b)).astype(F32).astype(BF16)
        picked = dot_nn(pick, refs[x, 0, span, :]).astype(BF16)
        for d in range(8):
            stage[d, j * 8 * ROWS : (j + 1) * 8 * ROWS, :] = picked[d * 8 * ROWS : (d + 1) * 8 * ROWS]
    for d in range(8):
        turned = dot_nn(swap_ref[...], stage[d]).astype(BF16)
        out_ref[d * 8 : (d + 1) * 8, 0] = turned.reshape(8, 8 * ROWS, HD)


def pack_first_kernel(routes_ref, rows_ref, swap_ref, packed_out, rho_out, stage):
    expert = lax.broadcasted_iota(jnp.int32, (EXPERTS, BLOCK), 0)
    before = (
        lax.broadcasted_iota(jnp.int32, (BLOCK, BLOCK), 0)
        < lax.broadcasted_iota(jnp.int32, (BLOCK, BLOCK), 1)
    ).astype(F32).astype(BF16)

    def row_of(e, slot):
        return (((e >> 1) & 7) * 8 + (e >> 4)) * ROWS + (e & 1) * CAP + slot

    def rho_of(x, span):
        first = routes_ref[x, 0, 0:1, span]
        second = routes_ref[x, 0, 1:2, span]
        hot_a = (expert == first).astype(F32)
        hot_b = (expert == second).astype(F32)
        earlier = dot_nn((hot_a + hot_b).astype(BF16), before)
        rho_a = row_of(first, jnp.sum(hot_a * earlier, axis=0, keepdims=True).astype(jnp.int32))
        rho_b = row_of(second, jnp.sum(hot_b * earlier, axis=0, keepdims=True).astype(jnp.int32))
        rho_out[x, 0, 0:1, span] = rho_a
        rho_out[x, 0, 1:2, span] = rho_b
        return rho_a, rho_b

    pack_rows(rows_ref, rho_of, swap_ref, packed_out, stage)


def pack_again_kernel(rho_ref, rows_ref, swap_ref, packed_out, stage):
    def rho_of(x, span):
        return rho_ref[x, 0, 0:1, span], rho_ref[x, 0, 1:2, span]

    pack_rows(rows_ref, rho_of, swap_ref, packed_out, stage)


def pack(kernel, ids, rows, swap, with_rho, first, steps):
    slab = pl.BlockSpec((4, 1, 2 * BLOCK, HD), lambda t: (0, t + first, 0, 0))
    packed = pl.BlockSpec((64, 1, 8 * ROWS, HD), lambda t: (0, t, 0, 0))
    id_spec = pl.BlockSpec((4, 1, TOP, 2 * BLOCK), lambda t: (0, t + first, 0, 0))
    shapes = [
        jax.ShapeDtypeStruct((64, steps, 8 * ROWS, HD), BF16),
        jax.ShapeDtypeStruct((4, 4, TOP, 2 * BLOCK), jnp.int32),
    ]
    return pl.pallas_call(
        kernel,
        grid=(steps,),
        in_specs=[id_spec, slab, pl.BlockSpec(swap.shape, lambda t: (0, 0))],
        out_specs=[packed, id_spec][: 1 + with_rho],
        out_shape=shapes[: 1 + with_rho],
        scratch_shapes=[pltpu.VMEM((8, 64 * ROWS, HD), BF16)],
        cost_estimate=pl.CostEstimate(flops=1000, bytes_accessed=1000, transcendentals=0),
        compiler_params=params(1),
        name="pack_rows",
    )(ids, rows, swap)


def second_expert(shape):
    return lax.rem(lax.broadcasted_iota(jnp.int32, shape, 0), ROWS) >= CAP


def head_kernel(grad_ref, w_ref, o0, o1, o2, o3):
    for g in range(2):
        total = jnp.zeros((32 * ROWS, EPD * HD), F32)
        for r in range(8):
            total += dot_nt(grad_ref[r, g], w_ref[r])
        own = jnp.where(second_expert((32 * ROWS, HD)), total[:, HD:], total[:, :HD])
        own = own.astype(BF16).reshape(4, 8 * ROWS, HD)
        for t, out in enumerate((o0, o1, o2, o3)):
            out[g] = own[t]


def head_sums(grad_rows, weights):
    return pl.pallas_call(
        head_kernel,
        grid=(4,),
        in_specs=[
            pl.BlockSpec((8, 2, 32 * ROWS, HD), lambda i: (0, i, 0, 0)),
            pl.BlockSpec((8, EPD * HD, HD), lambda i: (0, 0, 0)),
        ],
        out_specs=[pl.BlockSpec((2, 8 * ROWS, HD), lambda i: (i, 0, 0))] * 4,
        out_shape=[jax.ShapeDtypeStruct((8, 8 * ROWS, HD), BF16)] * 4,
        cost_estimate=pl.CostEstimate(flops=1000, bytes_accessed=1000, transcendentals=0),
        compiler_params=params(1),
        name="head_sums",
    )(grad_rows.reshape(8, 8, 32 * ROWS, HD), weights)


def address_kernel(t0, t1, t2, t3, pad_ref, out_ref):
    for t, part in enumerate((t0, t1, t2, t3)):
        rows = dot_nn(pad_ref[...], part[...]).astype(BF16)
        for x in range(4):
            out_ref[x, t] = rows[x * 16 * PAD : (x + 1) * 16 * PAD]


def address_heads(parts, pad):
    return pl.pallas_call(
        address_kernel,
        out_shape=jax.ShapeDtypeStruct((4, 4, 16 * PAD, HD), BF16),
        cost_estimate=pl.CostEstimate(flops=1000, bytes_accessed=1000, transcendentals=0),
        compiler_params=params(0),
        name="address_heads",
    )(*[p.reshape(64 * ROWS, HD) for p in parts], pad)


def forward_kernel(at_ref, q_ref, kv_ref, gate_ref, prob_out, head_out, gated_out, score):
    n, length = q_ref.shape[0], kv_ref.shape[0]
    step = 512
    q = q_ref[...]
    start = (at_ref[0] * 8 + at_ref[1] * 2 + at_ref[2]) * BLOCK
    pos = start + lax.rem(lax.broadcasted_iota(jnp.int32, (n, step), 0), BLOCK)
    lane = lax.broadcasted_iota(jnp.int32, (n, step), 1)
    top = jnp.full((n, 1), -jnp.inf, F32)
    for c in range(0, length, step):
        s = dot_nt(q, kv_ref[c : c + step, :HD]) * (1.0 / math.sqrt(HD))
        s = jnp.where(lane + c <= pos, s, -jnp.inf)
        score[:, c : c + step] = s
        top = jnp.maximum(top, jnp.max(s, axis=1, keepdims=True))
    total = jnp.zeros((n, 1), F32)
    for c in range(0, length, step):
        w = jnp.exp(score[:, c : c + step] - top)
        score[:, c : c + step] = w
        total += jnp.sum(w, axis=1, keepdims=True)
    inv = 1.0 / total
    out = jnp.zeros((n, HD), F32)
    for c in range(0, length, step):
        p = (score[:, c : c + step] * inv).astype(BF16)
        prob_out[:, c : c + step] = p
        out += dot_nn(p, kv_ref[c : c + step, HD:])
    head_out[...] = out
    gated_out[...] = (gate_ref[...] * out).astype(BF16)


def attend_forward(at, q, kv, gates):
    n, length = q.shape[0], kv.shape[0]
    vm = pl.BlockSpec(memory_space=pltpu.VMEM)
    return pl.pallas_call(
        forward_kernel,
        in_specs=[pl.BlockSpec(memory_space=pltpu.SMEM), vm, vm, vm],
        out_specs=[vm, vm, vm],
        out_shape=[
            jax.ShapeDtypeStruct((n, length), BF16),
            jax.ShapeDtypeStruct((n, HD), F32),
            jax.ShapeDtypeStruct((n, HD), BF16),
        ],
        scratch_shapes=[pltpu.VMEM((n, length), F32)],
        cost_estimate=pl.CostEstimate(flops=1000, bytes_accessed=1000, transcendentals=0),
        compiler_params=params(0),
        name="attend_forward",
    )(at, q, kv, gates)


def backward_kernel(
    head_ref, rho_row_ref, rho_col_ref, gate_ref, q_ref, kv_ref, prob_ref, out_ref, gated_ref, slots_out, dkv_out
):
    n, length = q_ref.shape[0], kv_ref.shape[0]
    step = 512
    scale = 1.0 / math.sqrt(HD)
    lanes = lax.broadcasted_iota(jnp.int32, (n, 256 * PAD), 1)
    lanes = (lanes >> 9) * (16 * PAD) + (lanes & (16 * PAD - 1))
    pick = (lanes == rho_col_ref[...]).astype(F32).astype(BF16)
    head_grad = gate_ref[...] * dot_nn(pick, head_ref[...])
    delta = jnp.sum(head_grad * out_ref[...], axis=1, keepdims=True)
    grad = head_grad.astype(BF16)
    q = q_ref[...]
    dq = jnp.zeros((n, HD), F32)
    for c in range(0, length, step):
        keys, values = kv_ref[c : c + step, :HD], kv_ref[c : c + step, HD:]
        p = prob_ref[:, c : c + step]
        ds = (p.astype(F32) * (dot_nt(grad, values) - delta)).astype(BF16)
        dq += dot_nn(ds, keys)
        dkv_out[c : c + step, :HD] = (dot_tn(ds, q) * scale).astype(BF16)
        dkv_out[c : c + step, HD:] = dot_tn(p, grad).astype(BF16)
    both = jnp.concatenate([(dq * scale).astype(BF16), gated_ref[...]], axis=1)
    rows = lax.broadcasted_iota(jnp.int32, (64 * PAD, n), 0)
    place = (rows == rho_row_ref[...]).astype(F32).astype(BF16)
    slots_out[...] = dot_nn(place, both).astype(BF16)


def attend_backward(head, rho_row, rho_col, gates, q, kv, prob, out, gated):
    return pl.pallas_call(
        backward_kernel,
        out_shape=[
            jax.ShapeDtypeStruct((64 * PAD, 2 * HD), BF16),
            jax.ShapeDtypeStruct(kv.shape, BF16),
        ],
        cost_estimate=pl.CostEstimate(flops=1000, bytes_accessed=1000, transcendentals=0),
        compiler_params=params(0),
        name="attend_backward",
    )(head, rho_row, rho_col, gates, q, kv, prob, out, gated)


def unpad_kernel(rows_ref, unpad_ref, out_ref):
    out_ref[...] = dot_nn(unpad_ref[...], rows_ref[...]).astype(BF16)


def unpad_rows(rows, unpad):
    return pl.pallas_call(
        unpad_kernel,
        out_shape=jax.ShapeDtypeStruct((64 * ROWS, 2 * HD), BF16),
        cost_estimate=pl.CostEstimate(flops=10000000000, bytes_accessed=4000000, transcendentals=0),
        compiler_params=params(0),
        name="unpad_rows",
    )(rows, unpad)


def by_expert(rows):
    later = second_expert(rows.shape)
    zero = jnp.zeros_like(rows)
    return jnp.concatenate([jnp.where(later, zero, rows), jnp.where(later, rows, zero)], axis=1)


def in_order(at_ref, parts, stage):
    zh = at_ref[1]
    for s, part in enumerate(parts):
        stage[(zh + 4 - s) % 4] = part[...]


def back_kernel(at_ref, a_ref, b_ref, c_ref, d_ref, w_ref, out_ref, dqg_ref):
    in_order(at_ref, (a_ref, b_ref, c_ref, d_ref), dqg_ref)
    for g in range(2):
        dq = by_expert(dqg_ref[:, g, :, :HD].reshape(32 * ROWS, HD))
        for r in range(8):
            w = jnp.concatenate([w_ref[r, 0], w_ref[r, 1]], axis=1)
            out_ref[r, g] = dot_nt(dq, w).astype(BF16)


def route_back(at, dqg, weights):
    return pl.pallas_call(
        back_kernel,
        grid=(4,),
        in_specs=[pl.BlockSpec(memory_space=pltpu.SMEM)]
        + [pl.BlockSpec((2, 8 * ROWS, 2 * HD), lambda i: (i, 0, 0))] * 4
        + [pl.BlockSpec((8, EPD, HD, HD), lambda i: (0, 0, 0, 0))],
        out_specs=pl.BlockSpec((8, 2, 32 * ROWS, HD), lambda i: (0, i, 0, 0)),
        out_shape=jax.ShapeDtypeStruct((8, 8, 32 * ROWS, HD), BF16),
        scratch_shapes=[pltpu.VMEM((4, 2, 8 * ROWS, 2 * HD), BF16)],
        cost_estimate=pl.CostEstimate(flops=1000, bytes_accessed=1000, transcendentals=0),
        compiler_params=params(1),
        name="route_back",
    )(at, *dqg, weights)


def early_weights_kernel(at_ref, a_ref, b_ref, c_ref, d_ref, hid_ref, grad_ref, wq_acc, wo_acc, dqg_ref):
    in_order(at_ref, (a_ref, b_ref, c_ref, d_ref), dqg_ref)

    @pl.when(pl.program_id(0) == 0)
    def _():
        wq_acc[...] = jnp.zeros_like(wq_acc)
        wo_acc[...] = jnp.zeros_like(wo_acc)

    for g in range(2):
        dq = by_expert(dqg_ref[:2, g, :, :HD].reshape(16 * ROWS, HD))
        gated = by_expert(dqg_ref[:, g, :, HD:].reshape(32 * ROWS, HD))
        for r in range(8):
            wq_acc[r] += dot_tn(hid_ref[r, g], dq)
            wo_acc[r] += dot_tn(gated, grad_ref[r, g])


def late_weights_kernel(at_ref, a_ref, b_ref, c_ref, d_ref, hid_ref, wq_ref, wo_ref, out_ref, dqg_ref, wq_acc):
    in_order(at_ref, (a_ref, b_ref, c_ref, d_ref), dqg_ref)

    @pl.when(pl.program_id(0) == 0)
    def _():
        wq_acc[...] = wq_ref[...]
        for r in range(8):
            for k in range(EPD):
                out_ref[r, k, 1] = wo_ref[r, k * HD : (k + 1) * HD, :].astype(BF16)

    for g in range(2):
        dq = by_expert(dqg_ref[2:, g, :, :HD].reshape(16 * ROWS, HD))
        for r in range(8):
            wq_acc[r] += dot_tn(hid_ref[r, g], dq)

    @pl.when(pl.program_id(0) == 3)
    def _():
        for r in range(8):
            for k in range(EPD):
                out_ref[r, k, 0] = wq_acc[r, :, k * HD : (k + 1) * HD].astype(BF16)


def weights_call(kernel, name, operands, in_specs, out_shapes, scratch):
    def whole(shape):
        return pl.BlockSpec(shape, lambda i: (0,) * len(shape))

    return pl.pallas_call(
        kernel,
        grid=(4,),
        in_specs=[pl.BlockSpec(memory_space=pltpu.SMEM)]
        + [pl.BlockSpec((2, 8 * ROWS, 2 * HD), lambda i: (i, 0, 0))] * 4
        + in_specs
        + [whole(o.shape) for o in operands[5 + len(in_specs) :]],
        out_specs=[whole(o.shape) for o in out_shapes],
        out_shape=out_shapes,
        scratch_shapes=[pltpu.VMEM((4, 2, 8 * ROWS, 2 * HD), BF16)] + scratch,
        cost_estimate=pl.CostEstimate(flops=1000, bytes_accessed=1000, transcendentals=0),
        compiler_params=params(1),
        name=name,
    )(*operands)


def early_weights(at, dqg, hid_a, grad_rows):
    return weights_call(
        early_weights_kernel,
        "early_weights",
        [at, *dqg, hid_a.reshape(8, 8, 16 * ROWS, HD), grad_rows.reshape(8, 8, 32 * ROWS, HD)],
        [
            pl.BlockSpec((8, 2, 16 * ROWS, HD), lambda i: (0, i, 0, 0)),
            pl.BlockSpec((8, 2, 32 * ROWS, HD), lambda i: (0, i, 0, 0)),
        ],
        [
            jax.ShapeDtypeStruct((8, HD, EPD * HD), F32),
            jax.ShapeDtypeStruct((8, EPD * HD, HD), F32),
        ],
        [],
    )


def late_weights(at, dqg, hid_b, wq, wo):
    (out,) = weights_call(
        late_weights_kernel,
        "late_weights",
        [at, *dqg, hid_b.reshape(8, 8, 16 * ROWS, HD), wq, wo],
        [pl.BlockSpec((8, 2, 16 * ROWS, HD), lambda i: (0, i, 0, 0))],
        [jax.ShapeDtypeStruct((8, EPD, 2, HD, HD), BF16)],
        [pltpu.VMEM((8, HD, EPD * HD), F32)],
    )
    return out


def projection_kernel(hid_ref, dkv_ref, out_ref):
    out_ref[...] = dot_tn(hid_ref[...], dkv_ref[...]).astype(BF16)


def projection(hid, dkv):
    return pl.pallas_call(
        projection_kernel,
        out_shape=jax.ShapeDtypeStruct((HD, 2 * HD), BF16),
        cost_estimate=pl.CostEstimate(flops=1000, bytes_accessed=1000, transcendentals=0),
        compiler_params=params(0),
        name="projection",
    )(hid, dkv)


def unpack_kernel(rho_ref, back_ref, swap_ref, out_ref, stage):
    for d in range(8):
        rows = back_ref[d * 8 : (d + 1) * 8, 0].reshape(64 * ROWS, HD)
        turned = dot_nn(swap_ref[...], rows).astype(BF16)
        for j in range(8):
            stage[j, d * 8 * ROWS : (d + 1) * 8 * ROWS, :] = turned[j * 8 * ROWS : (j + 1) * 8 * ROWS]
    row_id = lax.broadcasted_iota(jnp.int32, (64 * ROWS, BLOCK), 0)
    for j in range(8):
        x, span = j // 2, pl.ds((j % 2) * BLOCK, BLOCK)
        rho_a = rho_ref[x, 0, 0:1, span]
        rho_b = rho_ref[x, 0, 1:2, span]
        pick = ((row_id == rho_a) | (row_id == rho_b)).astype(F32).astype(BF16)
        out_ref[x, 0, span, :] = dot_tn(pick, stage[j])


def unpack(rho, back, swap):
    return pl.pallas_call(
        unpack_kernel,
        grid=(4,),
        in_specs=[
            pl.BlockSpec((4, 1, TOP, 2 * BLOCK), lambda t: (0, t, 0, 0)),
            pl.BlockSpec((64, 1, 8 * ROWS, HD), lambda t: (0, t, 0, 0)),
            pl.BlockSpec(swap.shape, lambda t: (0, 0)),
        ],
        out_specs=pl.BlockSpec((4, 1, 2 * BLOCK, HD), lambda t: (0, t, 0, 0)),
        out_shape=jax.ShapeDtypeStruct((4, 4, 2 * BLOCK, HD), F32),
        scratch_shapes=[pltpu.VMEM((8, 64 * ROWS, HD), BF16)],
        cost_estimate=pl.CostEstimate(flops=1000, bytes_accessed=1000, transcendentals=0),
        compiler_params=params(1),
        name="unpack_rows",
    )(rho, back, swap)


def finish_kernel(rows_ref, dkv_ref, wkv_ref, out_ref):
    for x in range(4):
        total = rows_ref[x, 0] + dot_nt(dkv_ref[x, 0], wkv_ref[...])
        out_ref[x, 0] = total.astype(BF16)


def finish(rows, dkv, wkv):
    return pl.pallas_call(
        finish_kernel,
        grid=(4,),
        in_specs=[
            pl.BlockSpec((4, 1, 2 * BLOCK, HD), lambda t: (0, t, 0, 0)),
            pl.BlockSpec((4, 1, 2 * BLOCK, 2 * HD), lambda t: (0, t, 0, 0)),
            pl.BlockSpec(wkv.shape, lambda t: (0, 0)),
        ],
        out_specs=pl.BlockSpec((4, 1, 2 * BLOCK, HD), lambda t: (0, t, 0, 0)),
        out_shape=jax.ShapeDtypeStruct((4, 4, 2 * BLOCK, HD), BF16),
        cost_estimate=pl.CostEstimate(flops=5000000000, bytes_accessed=10000000, transcendentals=0),
        compiler_params=params(1),
        name="finish_rows",
    )(rows, dkv, wkv)


def exchange(rows, axes):
    return lax.all_to_all(rows, axes, split_axis=0, concat_axis=0, tiled=True)


def shifted(rows, axis, s):
    n = lax.axis_size(axis)
    return lax.ppermute(rows, axis, [(i, (i + s) % n) for i in range(n)])


def gather(rows, axis):
    return [rows] + [shifted(rows, axis, s) for s in range(1, lax.axis_size(axis))]


def after(rows, *others):
    return lax.optimization_barrier((rows,) + others)[0]


def per_device(
    hidden, out_grad, queries, key_heads, value_heads, routes, route_gates, w_query, w_out, w_key, w_value
):
    swap, pad = swap_matrix().astype(BF16), pad_matrix().astype(BF16)
    unpad = pad.T
    xi, zh, zl = lax.axis_index("x"), lax.axis_index("zh"), lax.axis_index("zl")
    at = jnp.stack([xi, zh, zl])
    kv = lax.all_gather(jnp.concatenate([key_heads[0], value_heads[0]], axis=1), SEQ, axis=0, tiled=True)
    routes_t = routes[0].reshape(4, 4, 2 * BLOCK, TOP).transpose(0, 1, 3, 2)
    slab = (4, 4, 2 * BLOCK, HD)
    grad_packed, rho = pack(pack_first_kernel, routes_t, out_grad[0].reshape(slab), swap, 1, 0, 4)
    w_out_r = exchange(w_out, SLAB).reshape(8, EPD * HD, HD)
    grad_rows = exchange(after(grad_packed, w_out_r), WIDE)
    (hid_a,) = pack(pack_again_kernel, rho, hidden[0].reshape(slab), swap, 0, 0, 2)
    (hid_b,) = pack(pack_again_kernel, rho, hidden[0].reshape(slab), swap, 0, 2, 2)
    q = queries[0].transpose(1, 0, 2).reshape(TOP * BLOCK, HD)
    gates = route_gates[0].T.reshape(TOP * BLOCK, 1)
    own = lax.dynamic_slice(rho, (xi, zh, 0, zl * BLOCK), (1, 1, TOP, BLOCK)).reshape(TOP * BLOCK)
    own = own // ROWS * PAD + own % ROWS
    own_row, own_col = own.reshape(1, -1), own.reshape(-1, 1)

    parts = head_sums(after(grad_rows, own_row, own_col, q, gates, hid_a, hid_b), w_out_r)
    head_home = exchange(address_heads(parts, pad).reshape(256, PAD, HD), SEQ + GRP)
    hid_a = exchange(after(hid_a, head_home), WIDE)
    prob, head_out, gated = attend_forward(at, after(q, head_home), kv, gates)
    slots, dkv_part = attend_backward(
        head_home.reshape(256 * PAD, HD), own_row, own_col, gates, q, kv,
        prob, head_out, gated,
    )
    dkv_x = lax.psum_scatter(dkv_part, "x", scatter_dimension=0, tiled=True)
    mine = exchange(after(slots, hid_a).reshape(64, PAD, 2 * HD), WIDE).reshape(64 * PAD, 2 * HD)
    dqg = unpad_rows(mine, unpad).reshape(8, 8 * ROWS, 2 * HD)
    first = dqg
    dqg = gather(dqg, "zh")
    w_query_r = exchange(after(w_query, mine), SLAB).reshape(8, EPD, HD, HD)
    dkv_z = exchange(after(dkv_x, w_query_r, *dqg).reshape(8, BLOCK, 2 * HD), ("zh", "zl"))
    dkv_own = dkv_z.astype(F32).sum(axis=0).astype(BF16)
    dkv = lax.all_gather(dkv_own, SEQ, axis=0, tiled=True)
    back_rows = route_back(at, dqg, w_query_r).reshape(64, 4, 8 * ROWS, HD)
    back = exchange(after(back_rows, dkv_z), WIDE)
    hid_b = exchange(after(hid_b, back), WIDE)
    unpacked = unpack(rho, back, swap)
    dqg[0] = after(dqg[0], back_rows)
    wq, wo = early_weights(at, dqg, hid_a, grad_rows)
    dqg[0] = after(dqg[0], unpacked, wq)
    grads = late_weights(at, dqg, hid_b, wq, wo).reshape(16, 2, HD, HD)
    grads = exchange(grads, SLAB)
    grad_wq, grad_wo = grads[:, 0].astype(F32), grads[:, 1].astype(F32)

    wkv = jnp.concatenate([w_key, w_value], axis=1)
    proj = projection(hidden[0], dkv)
    grad_hidden = finish(unpacked, dkv.reshape(4, 4, 2 * BLOCK, 2 * HD), wkv).reshape(1, 4096, HD)
    proj = sum(p.astype(F32) for p in gather(proj, "dev")).astype(BF16)
    proj = [p.astype(F32) for p in gather(proj, "node")]
    proj[0] = after(proj[0], grad_hidden)
    proj = (proj[0] + proj[2]) + (proj[1] + proj[3])
    return (grad_hidden, grad_wq, grad_wo, proj[:, :HD], proj[:, HD:])


def solution(mesh):
    fine = Mesh(mesh.devices.reshape(4, 4, 2, 4, 2), SEQ + GRP)
    in_specs = (
        P(GRP, None, SEQ),
        P(GRP, None, SEQ),
        P(GRP, SEQ, None, None),
        P(GRP, SEQ, None),
        P(GRP, SEQ, None),
        P(GRP, None, None),
        P(GRP, SEQ, None),
        P(GRP, SEQ, None),
        P(GRP, None, SEQ),
        P(SEQ, None),
        P(SEQ, None),
    )
    out_specs = (
        P(GRP, None, SEQ),
        P(GRP, SEQ, None),
        P(GRP, None, SEQ),
        P(SEQ, None),
        P(SEQ, None),
    )
    return jax.shard_map(per_device, mesh=fine, in_specs=in_specs, out_specs=out_specs, check_vma=False)
```

```python
import math

import jax
import jax.numpy as jnp
import numpy as np
from jax import lax
from jax.experimental import pallas as pl
from jax.experimental.pallas import tpu as pltpu
from jax.sharding import Mesh
from jax.sharding import PartitionSpec as P

HD = 128
EXPERTS = 128
TOP = 2
CAP = 3
BLOCK = 128
EPD = 2
ROWS = EPD * CAP
PAD = 8
SEQ = ("x", "zh", "zl")
GRP = ("node", "dev")
SLAB = ("x", "zl")
WIDE = ("x", "zl", "node", "dev")
F32 = jnp.float32
BF16 = jnp.bfloat16
VMEM_LIMIT = 56 * 1024 * 1024


def swap_matrix():
    out = np.arange(8 * 8 * ROWS)
    a, b, q = out // (8 * ROWS), out // ROWS % 8, out % ROWS
    m = np.zeros((8 * 8 * ROWS, 8 * 8 * ROWS), np.float32)
    m[out, b * 8 * ROWS + a * ROWS + q] = 1
    return m


def pad_matrix():
    src = np.arange(8 * 8 * ROWS)
    a, b, q = src // (8 * ROWS), src // ROWS % 8, src % ROWS
    m = np.zeros((8 * 8 * PAD, 8 * 8 * ROWS), np.float32)
    m[b * 8 * PAD + a * PAD + q, src] = 1
    return m


def params(n):
    return pltpu.CompilerParams(dimension_semantics=("arbitrary",) * n, vmem_limit_bytes=VMEM_LIMIT)


def dot_nt(a, b):
    return lax.dot_general(a, b, (((1,), (1,)), ((), ())), preferred_element_type=F32)


def dot_tn(a, b):
    return lax.dot_general(a, b, (((0,), (0,)), ((), ())), preferred_element_type=F32)


def dot_nn(a, b):
    return jnp.dot(a, b, preferred_element_type=F32)


def pack_rows(refs, rho_of, swap_ref, out_ref, stage):
    row_id = lax.broadcasted_iota(jnp.int32, (64 * ROWS, BLOCK), 0)
    for j in range(8):
        x, span = j // 2, pl.ds((j % 2) * BLOCK, BLOCK)
        rho_a, rho_b = rho_of(x, span)
        pick = ((row_id == rho_a) | (row_id == rho_b)).astype(F32).astype(BF16)
        picked = dot_nn(pick, refs[x, 0, span, :]).astype(BF16)
        for d in range(8):
            stage[d, j * 8 * ROWS : (j + 1) * 8 * ROWS, :] = picked[d * 8 * ROWS : (d + 1) * 8 * ROWS]
    for d in range(8):
        turned = dot_nn(swap_ref[...], stage[d]).astype(BF16)
        out_ref[d * 8 : (d + 1) * 8, 0] = turned.reshape(8, 8 * ROWS, HD)


def pack_first_kernel(routes_ref, rows_ref, swap_ref, packed_out, rho_out, stage):
    expert = lax.broadcasted_iota(jnp.int32, (EXPERTS, BLOCK), 0)
    before = (
        lax.broadcasted_iota(jnp.int32, (BLOCK, BLOCK), 0)
        < lax.broadcasted_iota(jnp.int32, (BLOCK, BLOCK), 1)
    ).astype(F32).astype(BF16)

    def row_of(e, slot):
        return (((e >> 1) & 7) * 8 + (e >> 4)) * ROWS + (e & 1) * CAP + slot

    def rho_of(x, span):
        first = routes_ref[x, 0, 0:1, span]
        second = routes_ref[x, 0, 1:2, span]
        hot_a = (expert == first).astype(F32)
        hot_b = (expert == second).astype(F32)
        earlier = dot_nn((hot_a + hot_b).astype(BF16), before)
        rho_a = row_of(first, jnp.sum(hot_a * earlier, axis=0, keepdims=True).astype(jnp.int32))
        rho_b = row_of(second, jnp.sum(hot_b * earlier, axis=0, keepdims=True).astype(jnp.int32))
        rho_out[x, 0, 0:1, span] = rho_a
        rho_out[x, 0, 1:2, span] = rho_b
        return rho_a, rho_b

    pack_rows(rows_ref, rho_of, swap_ref, packed_out, stage)


def pack_again_kernel(rho_ref, rows_ref, swap_ref, packed_out, stage):
    def rho_of(x, span):
        return rho_ref[x, 0, 0:1, span], rho_ref[x, 0, 1:2, span]

    pack_rows(rows_ref, rho_of, swap_ref, packed_out, stage)


def pack(kernel, ids, rows, swap, with_rho, first, steps):
    slab = pl.BlockSpec((4, 1, 2 * BLOCK, HD), lambda t: (0, t + first, 0, 0))
    packed = pl.BlockSpec((64, 1, 8 * ROWS, HD), lambda t: (0, t, 0, 0))
    id_spec = pl.BlockSpec((4, 1, TOP, 2 * BLOCK), lambda t: (0, t + first, 0, 0))
    shapes = [
        jax.ShapeDtypeStruct((64, steps, 8 * ROWS, HD), BF16),
        jax.ShapeDtypeStruct((4, 4, TOP, 2 * BLOCK), jnp.int32),
    ]
    return pl.pallas_call(
        kernel,
        grid=(steps,),
        in_specs=[id_spec, slab, pl.BlockSpec(swap.shape, lambda t: (0, 0))],
        out_specs=[packed, id_spec][: 1 + with_rho],
        out_shape=shapes[: 1 + with_rho],
        scratch_shapes=[pltpu.VMEM((8, 64 * ROWS, HD), BF16)],
        cost_estimate=pl.CostEstimate(flops=1000, bytes_accessed=1000, transcendentals=0),
        compiler_params=params(1),
        name="pack_rows",
    )(ids, rows, swap)


def second_expert(shape):
    return lax.rem(lax.broadcasted_iota(jnp.int32, shape, 0), ROWS) >= CAP


def head_kernel(grad_ref, w_ref, o0, o1, o2, o3):
    for g in range(2):
        total = jnp.zeros((32 * ROWS, EPD * HD), F32)
        for r in range(8):
            total += dot_nt(grad_ref[r, g], w_ref[r])
        own = jnp.where(second_expert((32 * ROWS, HD)), total[:, HD:], total[:, :HD])
        own = own.astype(BF16).reshape(4, 8 * ROWS, HD)
        for t, out in enumerate((o0, o1, o2, o3)):
            out[g] = own[t]


def head_sums(grad_rows, weights):
    return pl.pallas_call(
        head_kernel,
        grid=(4,),
        in_specs=[
            pl.BlockSpec((8, 2, 32 * ROWS, HD), lambda i: (0, i, 0, 0)),
            pl.BlockSpec((8, EPD * HD, HD), lambda i: (0, 0, 0)),
        ],
        out_specs=[pl.BlockSpec((2, 8 * ROWS, HD), lambda i: (i, 0, 0))] * 4,
        out_shape=[jax.ShapeDtypeStruct((8, 8 * ROWS, HD), BF16)] * 4,
        cost_estimate=pl.CostEstimate(flops=1000, bytes_accessed=1000, transcendentals=0),
        compiler_params=params(1),
        name="head_sums",
    )(grad_rows.reshape(8, 8, 32 * ROWS, HD), weights)


def address_kernel(t0, t1, t2, t3, pad_ref, out_ref):
    for t, part in enumerate((t0, t1, t2, t3)):
        rows = dot_nn(pad_ref[...], part[...]).astype(BF16)
        for x in range(4):
            out_ref[x, t] = rows[x * 16 * PAD : (x + 1) * 16 * PAD]


def address_heads(parts, pad):
    return pl.pallas_call(
        address_kernel,
        out_shape=jax.ShapeDtypeStruct((4, 4, 16 * PAD, HD), BF16),
        cost_estimate=pl.CostEstimate(flops=1000, bytes_accessed=1000, transcendentals=0),
        compiler_params=params(0),
        name="address_heads",
    )(*[p.reshape(64 * ROWS, HD) for p in parts], pad)


def forward_kernel(at_ref, q_ref, kv_ref, gate_ref, prob_out, head_out, gated_out, score):
    n, length = q_ref.shape[0], kv_ref.shape[0]
    step = 512
    q = q_ref[...]
    start = (at_ref[0] * 8 + at_ref[1] * 2 + at_ref[2]) * BLOCK
    pos = start + lax.rem(lax.broadcasted_iota(jnp.int32, (n, step), 0), BLOCK)
    lane = lax.broadcasted_iota(jnp.int32, (n, step), 1)
    top = jnp.full((n, 1), -jnp.inf, F32)
    for c in range(0, length, step):
        s = dot_nt(q, kv_ref[c : c + step, :HD]) * (1.0 / math.sqrt(HD))
        s = jnp.where(lane + c <= pos, s, -jnp.inf)
        score[:, c : c + step] = s
        top = jnp.maximum(top, jnp.max(s, axis=1, keepdims=True))
    total = jnp.zeros((n, 1), F32)
    for c in range(0, length, step):
        w = jnp.exp(score[:, c : c + step] - top)
        score[:, c : c + step] = w
        total += jnp.sum(w, axis=1, keepdims=True)
    inv = 1.0 / total
    out = jnp.zeros((n, HD), F32)
    for c in range(0, length, step):
        p = (score[:, c : c + step] * inv).astype(BF16)
        prob_out[:, c : c + step] = p
        out += dot_nn(p, kv_ref[c : c + step, HD:])
    head_out[...] = out
    gated_out[...] = (gate_ref[...] * out).astype(BF16)


def attend_forward(at, q, kv, gates):
    n, length = q.shape[0], kv.shape[0]
    vm = pl.BlockSpec(memory_space=pltpu.VMEM)
    return pl.pallas_call(
        forward_kernel,
        in_specs=[pl.BlockSpec(memory_space=pltpu.SMEM), vm, vm, vm],
        out_specs=[vm, vm, vm],
        out_shape=[
            jax.ShapeDtypeStruct((n, length), BF16),
            jax.ShapeDtypeStruct((n, HD), F32),
            jax.ShapeDtypeStruct((n, HD), BF16),
        ],
        scratch_shapes=[pltpu.VMEM((n, length), F32)],
        cost_estimate=pl.CostEstimate(flops=1000, bytes_accessed=1000, transcendentals=0),
        compiler_params=params(0),
        name="attend_forward",
    )(at, q, kv, gates)


def backward_kernel(
    head_ref, rho_row_ref, rho_col_ref, gate_ref, q_ref, kv_ref, prob_ref, out_ref, gated_ref, slots_out, dkv_out
):
    n, length = q_ref.shape[0], kv_ref.shape[0]
    step = 512
    scale = 1.0 / math.sqrt(HD)
    lanes = lax.broadcasted_iota(jnp.int32, (n, 256 * PAD), 1)
    lanes = (lanes >> 9) * (16 * PAD) + (lanes & (16 * PAD - 1))
    pick = (lanes == rho_col_ref[...]).astype(F32).astype(BF16)
    head_grad = gate_ref[...] * dot_nn(pick, head_ref[...])
    delta = jnp.sum(head_grad * out_ref[...], axis=1, keepdims=True)
    grad = head_grad.astype(BF16)
    q = q_ref[...]
    dq = jnp.zeros((n, HD), F32)
    for c in range(0, length, step):
        keys, values = kv_ref[c : c + step, :HD], kv_ref[c : c + step, HD:]
        p = prob_ref[:, c : c + step]
        ds = (p.astype(F32) * (dot_nt(grad, values) - delta)).astype(BF16)
        dq += dot_nn(ds, keys)
        dkv_out[c : c + step, :HD] = (dot_tn(ds, q) * scale).astype(BF16)
        dkv_out[c : c + step, HD:] = dot_tn(p, grad).astype(BF16)
    both = jnp.concatenate([(dq * scale).astype(BF16), gated_ref[...]], axis=1)
    rows = lax.broadcasted_iota(jnp.int32, (64 * PAD, n), 0)
    place = (rows == rho_row_ref[...]).astype(F32).astype(BF16)
    slots_out[...] = dot_nn(place, both).astype(BF16)


def attend_backward(head, rho_row, rho_col, gates, q, kv, prob, out, gated):
    return pl.pallas_call(
        backward_kernel,
        out_shape=[
            jax.ShapeDtypeStruct((64 * PAD, 2 * HD), BF16),
            jax.ShapeDtypeStruct(kv.shape, BF16),
        ],
        cost_estimate=pl.CostEstimate(flops=1000, bytes_accessed=1000, transcendentals=0),
        compiler_params=params(0),
        name="attend_backward",
    )(head, rho_row, rho_col, gates, q, kv, prob, out, gated)


def unpad_kernel(rows_ref, unpad_ref, out_ref):
    out_ref[...] = dot_nn(unpad_ref[...], rows_ref[...]).astype(BF16)


def unpad_rows(rows, unpad):
    return pl.pallas_call(
        unpad_kernel,
        out_shape=jax.ShapeDtypeStruct((64 * ROWS, 2 * HD), BF16),
        cost_estimate=pl.CostEstimate(flops=10000000000, bytes_accessed=4000000, transcendentals=0),
        compiler_params=params(0),
        name="unpad_rows",
    )(rows, unpad)


def by_expert(rows):
    later = second_expert(rows.shape)
    zero = jnp.zeros_like(rows)
    return jnp.concatenate([jnp.where(later, zero, rows), jnp.where(later, rows, zero)], axis=1)


def in_order(at_ref, parts, stage):
    zh = at_ref[1]
    for s, part in enumerate(parts):
        stage[(zh + 4 - s) % 4] = part[...]


def back_kernel(at_ref, a_ref, b_ref, c_ref, d_ref, w_ref, out_ref, dqg_ref):
    in_order(at_ref, (a_ref, b_ref, c_ref, d_ref), dqg_ref)
    for g in range(2):
        dq = by_expert(dqg_ref[:, g, :, :HD].reshape(32 * ROWS, HD))
        for r in range(8):
            w = jnp.concatenate([w_ref[r, 0], w_ref[r, 1]], axis=1)
            out_ref[r, g] = dot_nt(dq, w).astype(BF16)


def route_back(at, dqg, weights):
    return pl.pallas_call(
        back_kernel,
        grid=(4,),
        in_specs=[pl.BlockSpec(memory_space=pltpu.SMEM)]
        + [pl.BlockSpec((2, 8 * ROWS, 2 * HD), lambda i: (i, 0, 0))] * 4
        + [pl.BlockSpec((8, EPD, HD, HD), lambda i: (0, 0, 0, 0))],
        out_specs=pl.BlockSpec((8, 2, 32 * ROWS, HD), lambda i: (0, i, 0, 0)),
        out_shape=jax.ShapeDtypeStruct((8, 8, 32 * ROWS, HD), BF16),
        scratch_shapes=[pltpu.VMEM((4, 2, 8 * ROWS, 2 * HD), BF16)],
        cost_estimate=pl.CostEstimate(flops=1000, bytes_accessed=1000, transcendentals=0),
        compiler_params=params(1),
        name="route_back",
    )(at, *dqg, weights)


def early_weights_kernel(at_ref, a_ref, b_ref, c_ref, d_ref, hid_ref, grad_ref, wq_acc, wo_acc, dqg_ref):
    in_order(at_ref, (a_ref, b_ref, c_ref, d_ref), dqg_ref)

    @pl.when(pl.program_id(0) == 0)
    def _():
        wq_acc[...] = jnp.zeros_like(wq_acc)
        wo_acc[...] = jnp.zeros_like(wo_acc)

    for g in range(2):
        dq = by_expert(dqg_ref[:2, g, :, :HD].reshape(16 * ROWS, HD))
        gated = by_expert(dqg_ref[:, g, :, HD:].reshape(32 * ROWS, HD))
        for r in range(8):
            wq_acc[r] += dot_tn(hid_ref[r, g], dq)
            wo_acc[r] += dot_tn(gated, grad_ref[r, g])


def late_weights_kernel(at_ref, a_ref, b_ref, c_ref, d_ref, hid_ref, wq_ref, wo_ref, out_ref, dqg_ref, wq_acc):
    in_order(at_ref, (a_ref, b_ref, c_ref, d_ref), dqg_ref)

    @pl.when(pl.program_id(0) == 0)
    def _():
        wq_acc[...] = wq_ref[...]
        for r in range(8):
            for k in range(EPD):
                out_ref[r, k, 1] = wo_ref[r, k * HD : (k + 1) * HD, :].astype(BF16)

    for g in range(2):
        dq = by_expert(dqg_ref[2:, g, :, :HD].reshape(16 * ROWS, HD))
        for r in range(8):
            wq_acc[r] += dot_tn(hid_ref[r, g], dq)

    @pl.when(pl.program_id(0) == 3)
    def _():
        for r in range(8):
            for k in range(EPD):
                out_ref[r, k, 0] = wq_acc[r, :, k * HD : (k + 1) * HD].astype(BF16)


def weights_call(kernel, name, operands, in_specs, out_shapes, scratch):
    def whole(shape):
        return pl.BlockSpec(shape, lambda i: (0,) * len(shape))

    return pl.pallas_call(
        kernel,
        grid=(4,),
        in_specs=[pl.BlockSpec(memory_space=pltpu.SMEM)]
        + [pl.BlockSpec((2, 8 * ROWS, 2 * HD), lambda i: (i, 0, 0))] * 4
        + in_specs
        + [whole(o.shape) for o in operands[5 + len(in_specs) :]],
        out_specs=[whole(o.shape) for o in out_shapes],
        out_shape=out_shapes,
        scratch_shapes=[pltpu.VMEM((4, 2, 8 * ROWS, 2 * HD), BF16)] + scratch,
        cost_estimate=pl.CostEstimate(flops=1000, bytes_accessed=1000, transcendentals=0),
        compiler_params=params(1),
        name=name,
    )(*operands)


def early_weights(at, dqg, hid_a, grad_rows):
    return weights_call(
        early_weights_kernel,
        "early_weights",
        [at, *dqg, hid_a.reshape(8, 8, 16 * ROWS, HD), grad_rows.reshape(8, 8, 32 * ROWS, HD)],
        [
            pl.BlockSpec((8, 2, 16 * ROWS, HD), lambda i: (0, i, 0, 0)),
            pl.BlockSpec((8, 2, 32 * ROWS, HD), lambda i: (0, i, 0, 0)),
        ],
        [
            jax.ShapeDtypeStruct((8, HD, EPD * HD), F32),
            jax.ShapeDtypeStruct((8, EPD * HD, HD), F32),
        ],
        [],
    )


def late_weights(at, dqg, hid_b, wq, wo):
    (out,) = weights_call(
        late_weights_kernel,
        "late_weights",
        [at, *dqg, hid_b.reshape(8, 8, 16 * ROWS, HD), wq, wo],
        [pl.BlockSpec((8, 2, 16 * ROWS, HD), lambda i: (0, i, 0, 0))],
        [jax.ShapeDtypeStruct((8, EPD, 2, HD, HD), BF16)],
        [pltpu.VMEM((8, HD, EPD * HD), F32)],
    )
    return out


def projection_kernel(hid_ref, dkv_ref, out_ref):
    out_ref[...] = dot_tn(hid_ref[...], dkv_ref[...]).astype(BF16)


def projection(hid, dkv):
    return pl.pallas_call(
        projection_kernel,
        out_shape=jax.ShapeDtypeStruct((HD, 2 * HD), BF16),
        cost_estimate=pl.CostEstimate(flops=80000000000, bytes_accessed=1000, transcendentals=0),
        compiler_params=params(0),
        name="projection",
    )(hid, dkv)


def unpack_kernel(rho_ref, back_ref, swap_ref, out_ref, stage):
    for d in range(8):
        rows = back_ref[d * 8 : (d + 1) * 8, 0].reshape(64 * ROWS, HD)
        turned = dot_nn(swap_ref[...], rows).astype(BF16)
        for j in range(8):
            stage[j, d * 8 * ROWS : (d + 1) * 8 * ROWS, :] = turned[j * 8 * ROWS : (j + 1) * 8 * ROWS]
    row_id = lax.broadcasted_iota(jnp.int32, (64 * ROWS, BLOCK), 0)
    for j in range(8):
        x, span = j // 2, pl.ds((j % 2) * BLOCK, BLOCK)
        rho_a = rho_ref[x, 0, 0:1, span]
        rho_b = rho_ref[x, 0, 1:2, span]
        pick = ((row_id == rho_a) | (row_id == rho_b)).astype(F32).astype(BF16)
        out_ref[x, 0, span, :] = dot_tn(pick, stage[j])


def unpack(rho, back, swap):
    return pl.pallas_call(
        unpack_kernel,
        grid=(4,),
        in_specs=[
            pl.BlockSpec((4, 1, TOP, 2 * BLOCK), lambda t: (0, t, 0, 0)),
            pl.BlockSpec((64, 1, 8 * ROWS, HD), lambda t: (0, t, 0, 0)),
            pl.BlockSpec(swap.shape, lambda t: (0, 0)),
        ],
        out_specs=pl.BlockSpec((4, 1, 2 * BLOCK, HD), lambda t: (0, t, 0, 0)),
        out_shape=jax.ShapeDtypeStruct((4, 4, 2 * BLOCK, HD), F32),
        scratch_shapes=[pltpu.VMEM((8, 64 * ROWS, HD), BF16)],
        cost_estimate=pl.CostEstimate(flops=1000, bytes_accessed=1000, transcendentals=0),
        compiler_params=params(1),
        name="unpack_rows",
    )(rho, back, swap)


def finish_kernel(rows_ref, dkv_ref, wkv_ref, out_ref):
    for x in range(4):
        total = rows_ref[x, 0] + dot_nt(dkv_ref[x, 0], wkv_ref[...])
        out_ref[x, 0] = total.astype(BF16)


def finish(rows, dkv, wkv):
    return pl.pallas_call(
        finish_kernel,
        grid=(4,),
        in_specs=[
            pl.BlockSpec((4, 1, 2 * BLOCK, HD), lambda t: (0, t, 0, 0)),
            pl.BlockSpec((4, 1, 2 * BLOCK, 2 * HD), lambda t: (0, t, 0, 0)),
            pl.BlockSpec(wkv.shape, lambda t: (0, 0)),
        ],
        out_specs=pl.BlockSpec((4, 1, 2 * BLOCK, HD), lambda t: (0, t, 0, 0)),
        out_shape=jax.ShapeDtypeStruct((4, 4, 2 * BLOCK, HD), BF16),
        cost_estimate=pl.CostEstimate(flops=5000000000, bytes_accessed=10000000, transcendentals=0),
        compiler_params=params(1),
        name="finish_rows",
    )(rows, dkv, wkv)


def exchange(rows, axes):
    return lax.all_to_all(rows, axes, split_axis=0, concat_axis=0, tiled=True)


def shifted(rows, axis, s):
    n = lax.axis_size(axis)
    return lax.ppermute(rows, axis, [(i, (i + s) % n) for i in range(n)])


def gather(rows, axis):
    return [rows] + [shifted(rows, axis, s) for s in range(1, lax.axis_size(axis))]


def after(rows, *others):
    return lax.optimization_barrier((rows,) + others)[0]


def per_device(
    hidden, out_grad, queries, key_heads, value_heads, routes, route_gates, w_query, w_out, w_key, w_value
):
    swap, pad = swap_matrix().astype(BF16), pad_matrix().astype(BF16)
    unpad = pad.T
    xi, zh, zl = lax.axis_index("x"), lax.axis_index("zh"), lax.axis_index("zl")
    at = jnp.stack([xi, zh, zl])
    kv = lax.all_gather(jnp.concatenate([key_heads[0], value_heads[0]], axis=1), SEQ, axis=0, tiled=True)
    routes_t = routes[0].reshape(4, 4, 2 * BLOCK, TOP).transpose(0, 1, 3, 2)
    slab = (4, 4, 2 * BLOCK, HD)
    grad_packed, rho = pack(pack_first_kernel, routes_t, out_grad[0].reshape(slab), swap, 1, 0, 4)
    w_out_r = exchange(w_out, SLAB).reshape(8, EPD * HD, HD)
    grad_rows = exchange(after(grad_packed, w_out_r), WIDE)
    (hid_a,) = pack(pack_again_kernel, rho, hidden[0].reshape(slab), swap, 0, 0, 2)
    (hid_b,) = pack(pack_again_kernel, rho, hidden[0].reshape(slab), swap, 0, 2, 2)
    q = queries[0].transpose(1, 0, 2).reshape(TOP * BLOCK, HD)
    gates = route_gates[0].T.reshape(TOP * BLOCK, 1)
    own = lax.dynamic_slice(rho, (xi, zh, 0, zl * BLOCK), (1, 1, TOP, BLOCK)).reshape(TOP * BLOCK)
    own = own // ROWS * PAD + own % ROWS
    own_row, own_col = own.reshape(1, -1), own.reshape(-1, 1)

    parts = head_sums(after(grad_rows, own_row, own_col, q, gates, hid_a, hid_b), w_out_r)
    head_home = exchange(address_heads(parts, pad).reshape(256, PAD, HD), SEQ + GRP)
    hid_a = exchange(after(hid_a, head_home), WIDE)
    prob, head_out, gated = attend_forward(at, after(q, head_home), kv, gates)
    slots, dkv_part = attend_backward(
        head_home.reshape(256 * PAD, HD), own_row, own_col, gates, q, kv,
        prob, head_out, gated,
    )
    dkv_x = lax.psum_scatter(dkv_part, "x", scatter_dimension=0, tiled=True)
    mine = exchange(after(slots, hid_a).reshape(64, PAD, 2 * HD), WIDE).reshape(64 * PAD, 2 * HD)
    dqg = unpad_rows(mine, unpad).reshape(8, 8 * ROWS, 2 * HD)
    dqg = gather(dqg, "zh")
    dkv_z = exchange(after(dkv_x, *dqg).reshape(8, BLOCK, 2 * HD), ("zh", "zl"))
    dkv_own = dkv_z.astype(F32).sum(axis=0).astype(BF16)
    dkv = lax.all_gather(dkv_own, SEQ, axis=0, tiled=True)
    proj = projection(hidden[0], dkv)
    hid_b = exchange(after(hid_b, dkv_own), WIDE)
    wq, wo = early_weights(at, dqg, hid_a, grad_rows)
    w_query_r = exchange(after(w_query, hid_b, wq), SLAB).reshape(8, EPD, HD, HD)
    back_rows = route_back(at, dqg, w_query_r).reshape(64, 4, 8 * ROWS, HD)
    back = exchange(back_rows, WIDE)
    dqg[0] = after(dqg[0], back_rows)
    grads = late_weights(at, dqg, hid_b, wq, wo).reshape(16, 2, HD, HD)
    grads = exchange(after(grads, back, proj), SLAB)
    grad_wq, grad_wo = grads[:, 0].astype(F32), grads[:, 1].astype(F32)

    wkv = jnp.concatenate([w_key, w_value], axis=1)
    unpacked = unpack(rho, after(back, proj), swap)
    grad_hidden = finish(unpacked, dkv.reshape(4, 4, 2 * BLOCK, 2 * HD), wkv).reshape(1, 4096, HD)
    proj = sum(p.astype(F32) for p in gather(proj, "dev")).astype(BF16)
    proj = [p.astype(F32) for p in gather(proj, "node")]
    proj[0] = after(proj[0], grad_hidden)
    proj = (proj[0] + proj[2]) + (proj[1] + proj[3])
    return (grad_hidden, grad_wq, grad_wo, proj[:, :HD], proj[:, HD:])


def solution(mesh):
    fine = Mesh(mesh.devices.reshape(4, 4, 2, 4, 2), SEQ + GRP)
    in_specs = (
        P(GRP, None, SEQ),
        P(GRP, None, SEQ),
        P(GRP, SEQ, None, None),
        P(GRP, SEQ, None),
        P(GRP, SEQ, None),
        P(GRP, None, None),
        P(GRP, SEQ, None),
        P(GRP, SEQ, None),
        P(GRP, None, SEQ),
        P(SEQ, None),
        P(SEQ, None),
    )
    out_specs = (
        P(GRP, None, SEQ),
        P(GRP, SEQ, None),
        P(GRP, None, SEQ),
        P(SEQ, None),
        P(SEQ, None),
    )
    return jax.shard_map(per_device, mesh=fine, in_specs=in_specs, out_specs=out_specs, check_vma=False)
```

```python
import math

import jax
import jax.numpy as jnp
import numpy as np
from jax import lax
from jax.experimental import pallas as pl
from jax.experimental.pallas import tpu as pltpu
from jax.sharding import Mesh
from jax.sharding import PartitionSpec as P

HD = 128
EXPERTS = 128
TOP = 2
CAP = 3
BLOCK = 128
EPD = 2
ROWS = EPD * CAP
PAD = 8
SEQ = ("x", "zh", "zl")
GRP = ("node", "dev")
SLAB = ("x", "zl")
WIDE = ("x", "zl", "node", "dev")
F32 = jnp.float32
BF16 = jnp.bfloat16
VMEM_LIMIT = 56 * 1024 * 1024


def swap_matrix():
    out = np.arange(8 * 8 * ROWS)
    a, b, q = out // (8 * ROWS), out // ROWS % 8, out % ROWS
    m = np.zeros((8 * 8 * ROWS, 8 * 8 * ROWS), np.float32)
    m[out, b * 8 * ROWS + a * ROWS + q] = 1
    return m


def pad_matrix():
    src = np.arange(8 * 8 * ROWS)
    a, b, q = src // (8 * ROWS), src // ROWS % 8, src % ROWS
    m = np.zeros((8 * 8 * PAD, 8 * 8 * ROWS), np.float32)
    m[b * 8 * PAD + a * PAD + q, src] = 1
    return m


def params(n):
    return pltpu.CompilerParams(dimension_semantics=("arbitrary",) * n, vmem_limit_bytes=VMEM_LIMIT)


def dot_nt(a, b):
    return lax.dot_general(a, b, (((1,), (1,)), ((), ())), preferred_element_type=F32)


def dot_tn(a, b):
    return lax.dot_general(a, b, (((0,), (0,)), ((), ())), preferred_element_type=F32)


def dot_nn(a, b):
    return jnp.dot(a, b, preferred_element_type=F32)


def pack_rows(refs, rho_of, swap_ref, out_ref, stage):
    row_id = lax.broadcasted_iota(jnp.int32, (64 * ROWS, BLOCK), 0)
    for j in range(8):
        x, span = j // 2, pl.ds((j % 2) * BLOCK, BLOCK)
        rho_a, rho_b = rho_of(x, span)
        pick = ((row_id == rho_a) | (row_id == rho_b)).astype(F32).astype(BF16)
        picked = dot_nn(pick, refs[x, 0, span, :]).astype(BF16)
        for d in range(8):
            stage[d, j * 8 * ROWS : (j + 1) * 8 * ROWS, :] = picked[d * 8 * ROWS : (d + 1) * 8 * ROWS]
    for d in range(8):
        turned = dot_nn(swap_ref[...], stage[d]).astype(BF16)
        out_ref[d * 8 : (d + 1) * 8, 0] = turned.reshape(8, 8 * ROWS, HD)


def pack_first_kernel(routes_ref, rows_ref, swap_ref, packed_out, rho_out, stage):
    expert = lax.broadcasted_iota(jnp.int32, (EXPERTS, BLOCK), 0)
    before = (
        lax.broadcasted_iota(jnp.int32, (BLOCK, BLOCK), 0)
        < lax.broadcasted_iota(jnp.int32, (BLOCK, BLOCK), 1)
    ).astype(F32).astype(BF16)

    def row_of(e, slot):
        return (((e >> 1) & 7) * 8 + (e >> 4)) * ROWS + (e & 1) * CAP + slot

    def rho_of(x, span):
        first = routes_ref[x, 0, 0:1, span]
        second = routes_ref[x, 0, 1:2, span]
        hot_a = (expert == first).astype(F32)
        hot_b = (expert == second).astype(F32)
        earlier = dot_nn((hot_a + hot_b).astype(BF16), before)
        rho_a = row_of(first, jnp.sum(hot_a * earlier, axis=0, keepdims=True).astype(jnp.int32))
        rho_b = row_of(second, jnp.sum(hot_b * earlier, axis=0, keepdims=True).astype(jnp.int32))
        rho_out[x, 0, 0:1, span] = rho_a
        rho_out[x, 0, 1:2, span] = rho_b
        return rho_a, rho_b

    pack_rows(rows_ref, rho_of, swap_ref, packed_out, stage)


def pack_again_kernel(rho_ref, rows_ref, swap_ref, packed_out, stage):
    def rho_of(x, span):
        return rho_ref[x, 0, 0:1, span], rho_ref[x, 0, 1:2, span]

    pack_rows(rows_ref, rho_of, swap_ref, packed_out, stage)


def pack(kernel, ids, rows, swap, with_rho, first, steps):
    slab = pl.BlockSpec((4, 1, 2 * BLOCK, HD), lambda t: (0, t + first, 0, 0))
    packed = pl.BlockSpec((64, 1, 8 * ROWS, HD), lambda t: (0, t, 0, 0))
    id_spec = pl.BlockSpec((4, 1, TOP, 2 * BLOCK), lambda t: (0, t + first, 0, 0))
    shapes = [
        jax.ShapeDtypeStruct((64, steps, 8 * ROWS, HD), BF16),
        jax.ShapeDtypeStruct((4, 4, TOP, 2 * BLOCK), jnp.int32),
    ]
    return pl.pallas_call(
        kernel,
        grid=(steps,),
        in_specs=[id_spec, slab, pl.BlockSpec(swap.shape, lambda t: (0, 0))],
        out_specs=[packed, id_spec][: 1 + with_rho],
        out_shape=shapes[: 1 + with_rho],
        scratch_shapes=[pltpu.VMEM((8, 64 * ROWS, HD), BF16)],
        cost_estimate=pl.CostEstimate(flops=1000, bytes_accessed=1000, transcendentals=0),
        compiler_params=params(1),
        name="pack_rows",
    )(ids, rows, swap)


def second_expert(shape):
    return lax.rem(lax.broadcasted_iota(jnp.int32, shape, 0), ROWS) >= CAP


def head_kernel(grad_ref, w_ref, o0, o1, o2, o3):
    for g in range(2):
        total = jnp.zeros((32 * ROWS, EPD * HD), F32)
        for r in range(8):
            total += dot_nt(grad_ref[r, g], w_ref[r])
        own = jnp.where(second_expert((32 * ROWS, HD)), total[:, HD:], total[:, :HD])
        own = own.astype(BF16).reshape(4, 8 * ROWS, HD)
        for t, out in enumerate((o0, o1, o2, o3)):
            out[g] = own[t]


def head_sums(grad_rows, weights):
    return pl.pallas_call(
        head_kernel,
        grid=(4,),
        in_specs=[
            pl.BlockSpec((8, 2, 32 * ROWS, HD), lambda i: (0, i, 0, 0)),
            pl.BlockSpec((8, EPD * HD, HD), lambda i: (0, 0, 0)),
        ],
        out_specs=[pl.BlockSpec((2, 8 * ROWS, HD), lambda i: (i, 0, 0))] * 4,
        out_shape=[jax.ShapeDtypeStruct((8, 8 * ROWS, HD), BF16)] * 4,
        cost_estimate=pl.CostEstimate(flops=1000, bytes_accessed=1000, transcendentals=0),
        compiler_params=params(1),
        name="head_sums",
    )(grad_rows.reshape(8, 8, 32 * ROWS, HD), weights)


def address_kernel(t0, t1, t2, t3, pad_ref, out_ref):
    for t, part in enumerate((t0, t1, t2, t3)):
        rows = dot_nn(pad_ref[...], part[...]).astype(BF16)
        for x in range(4):
            out_ref[x, t] = rows[x * 16 * PAD : (x + 1) * 16 * PAD]


def address_heads(parts, pad):
    return pl.pallas_call(
        address_kernel,
        out_shape=jax.ShapeDtypeStruct((4, 4, 16 * PAD, HD), BF16),
        cost_estimate=pl.CostEstimate(flops=1000, bytes_accessed=1000, transcendentals=0),
        compiler_params=params(0),
        name="address_heads",
    )(*[p.reshape(64 * ROWS, HD) for p in parts], pad)


def forward_kernel(at_ref, q_ref, kv_ref, gate_ref, prob_out, head_out, gated_out, score):
    n, length = q_ref.shape[0], kv_ref.shape[0]
    step = 512
    q = q_ref[...]
    start = (at_ref[0] * 8 + at_ref[1] * 2 + at_ref[2]) * BLOCK
    pos = start + lax.rem(lax.broadcasted_iota(jnp.int32, (n, step), 0), BLOCK)
    lane = lax.broadcasted_iota(jnp.int32, (n, step), 1)
    top = jnp.full((n, 1), -jnp.inf, F32)
    for c in range(0, length, step):
        s = dot_nt(q, kv_ref[c : c + step, :HD]) * (1.0 / math.sqrt(HD))
        s = jnp.where(lane + c <= pos, s, -jnp.inf)
        score[:, c : c + step] = s
        top = jnp.maximum(top, jnp.max(s, axis=1, keepdims=True))
    total = jnp.zeros((n, 1), F32)
    for c in range(0, length, step):
        w = jnp.exp(score[:, c : c + step] - top)
        score[:, c : c + step] = w
        total += jnp.sum(w, axis=1, keepdims=True)
    inv = 1.0 / total
    out = jnp.zeros((n, HD), F32)
    for c in range(0, length, step):
        p = (score[:, c : c + step] * inv).astype(BF16)
        prob_out[:, c : c + step] = p
        out += dot_nn(p, kv_ref[c : c + step, HD:])
    head_out[...] = out
    gated_out[...] = (gate_ref[...] * out).astype(BF16)


def attend_forward(at, q, kv, gates):
    n, length = q.shape[0], kv.shape[0]
    vm = pl.BlockSpec(memory_space=pltpu.VMEM)
    return pl.pallas_call(
        forward_kernel,
        in_specs=[pl.BlockSpec(memory_space=pltpu.SMEM), vm, vm, vm],
        out_specs=[vm, vm, vm],
        out_shape=[
            jax.ShapeDtypeStruct((n, length), BF16),
            jax.ShapeDtypeStruct((n, HD), F32),
            jax.ShapeDtypeStruct((n, HD), BF16),
        ],
        scratch_shapes=[pltpu.VMEM((n, length), F32)],
        cost_estimate=pl.CostEstimate(flops=1000, bytes_accessed=1000, transcendentals=0),
        compiler_params=params(0),
        name="attend_forward",
    )(at, q, kv, gates)


def backward_kernel(
    head_ref, rho_row_ref, rho_col_ref, gate_ref, q_ref, kv_ref, prob_ref, out_ref, gated_ref, slots_out, dkv_out
):
    n, length = q_ref.shape[0], kv_ref.shape[0]
    step = 512
    scale = 1.0 / math.sqrt(HD)
    lanes = lax.broadcasted_iota(jnp.int32, (n, 256 * PAD), 1)
    lanes = (lanes >> 9) * (16 * PAD) + (lanes & (16 * PAD - 1))
    pick = (lanes == rho_col_ref[...]).astype(F32).astype(BF16)
    head_grad = gate_ref[...] * dot_nn(pick, head_ref[...])
    delta = jnp.sum(head_grad * out_ref[...], axis=1, keepdims=True)
    grad = head_grad.astype(BF16)
    q = q_ref[...]
    dq = jnp.zeros((n, HD), F32)
    for c in range(0, length, step):
        keys, values = kv_ref[c : c + step, :HD], kv_ref[c : c + step, HD:]
        p = prob_ref[:, c : c + step]
        ds = (p.astype(F32) * (dot_nt(grad, values) - delta)).astype(BF16)
        dq += dot_nn(ds, keys)
        dkv_out[c : c + step, :HD] = (dot_tn(ds, q) * scale).astype(BF16)
        dkv_out[c : c + step, HD:] = dot_tn(p, grad).astype(BF16)
    both = jnp.concatenate([(dq * scale).astype(BF16), gated_ref[...]], axis=1)
    rows = lax.broadcasted_iota(jnp.int32, (64 * PAD, n), 0)
    place = (rows == rho_row_ref[...]).astype(F32).astype(BF16)
    slots_out[...] = dot_nn(place, both).astype(BF16)


def attend_backward(head, rho_row, rho_col, gates, q, kv, prob, out, gated):
    return pl.pallas_call(
        backward_kernel,
        out_shape=[
            jax.ShapeDtypeStruct((64 * PAD, 2 * HD), BF16),
            jax.ShapeDtypeStruct(kv.shape, BF16),
        ],
        cost_estimate=pl.CostEstimate(flops=1000, bytes_accessed=1000, transcendentals=0),
        compiler_params=params(0),
        name="attend_backward",
    )(head, rho_row, rho_col, gates, q, kv, prob, out, gated)


def unpad_kernel(rows_ref, unpad_ref, out_ref):
    out_ref[...] = dot_nn(unpad_ref[...], rows_ref[...]).astype(BF16)


def unpad_rows(rows, unpad):
    return pl.pallas_call(
        unpad_kernel,
        out_shape=jax.ShapeDtypeStruct((64 * ROWS, 2 * HD), BF16),
        cost_estimate=pl.CostEstimate(flops=10000000000, bytes_accessed=4000000, transcendentals=0),
        compiler_params=params(0),
        name="unpad_rows",
    )(rows, unpad)


def by_expert(rows):
    later = second_expert(rows.shape)
    zero = jnp.zeros_like(rows)
    return jnp.concatenate([jnp.where(later, zero, rows), jnp.where(later, rows, zero)], axis=1)


def in_order(at_ref, parts, stage):
    zh = at_ref[1]
    for s, part in enumerate(parts):
        stage[(zh + 4 - s) % 4] = part[...]


def back_kernel(at_ref, a_ref, b_ref, c_ref, d_ref, w_ref, out_ref, dqg_ref):
    in_order(at_ref, (a_ref, b_ref, c_ref, d_ref), dqg_ref)
    for g in range(2):
        dq = by_expert(dqg_ref[:, g, :, :HD].reshape(32 * ROWS, HD))
        for r in range(8):
            w = jnp.concatenate([w_ref[r, 0], w_ref[r, 1]], axis=1)
            out_ref[r, g] = dot_nt(dq, w).astype(BF16)


def route_back(at, dqg, weights):
    return pl.pallas_call(
        back_kernel,
        grid=(4,),
        in_specs=[pl.BlockSpec(memory_space=pltpu.SMEM)]
        + [pl.BlockSpec((2, 8 * ROWS, 2 * HD), lambda i: (i, 0, 0))] * 4
        + [pl.BlockSpec((8, EPD, HD, HD), lambda i: (0, 0, 0, 0))],
        out_specs=pl.BlockSpec((8, 2, 32 * ROWS, HD), lambda i: (0, i, 0, 0)),
        out_shape=jax.ShapeDtypeStruct((8, 8, 32 * ROWS, HD), BF16),
        scratch_shapes=[pltpu.VMEM((4, 2, 8 * ROWS, 2 * HD), BF16)],
        cost_estimate=pl.CostEstimate(flops=1000, bytes_accessed=1000, transcendentals=0),
        compiler_params=params(1),
        name="route_back",
    )(at, *dqg, weights)


def early_weights_kernel(at_ref, a_ref, b_ref, c_ref, d_ref, hid_ref, grad_ref, wq_acc, wo_acc, dqg_ref):
    in_order(at_ref, (a_ref, b_ref, c_ref, d_ref), dqg_ref)

    @pl.when(pl.program_id(0) == 0)
    def _():
        wq_acc[...] = jnp.zeros_like(wq_acc)
        wo_acc[...] = jnp.zeros_like(wo_acc)

    for g in range(2):
        dq = by_expert(dqg_ref[:2, g, :, :HD].reshape(16 * ROWS, HD))
        gated = by_expert(dqg_ref[:, g, :, HD:].reshape(32 * ROWS, HD))
        for r in range(8):
            wq_acc[r] += dot_tn(hid_ref[r, g], dq)
            wo_acc[r] += dot_tn(gated, grad_ref[r, g])


def late_weights_kernel(at_ref, a_ref, b_ref, c_ref, d_ref, hid_ref, wq_ref, wo_ref, out_ref, dqg_ref, wq_acc):
    in_order(at_ref, (a_ref, b_ref, c_ref, d_ref), dqg_ref)

    @pl.when(pl.program_id(0) == 0)
    def _():
        wq_acc[...] = wq_ref[...]
        for r in range(8):
            for k in range(EPD):
                out_ref[r, k, 1] = wo_ref[r, k * HD : (k + 1) * HD, :].astype(BF16)

    for g in range(2):
        dq = by_expert(dqg_ref[2:, g, :, :HD].reshape(16 * ROWS, HD))
        for r in range(8):
            wq_acc[r] += dot_tn(hid_ref[r, g], dq)

    @pl.when(pl.program_id(0) == 3)
    def _():
        for r in range(8):
            for k in range(EPD):
                out_ref[r, k, 0] = wq_acc[r, :, k * HD : (k + 1) * HD].astype(BF16)


def weights_call(kernel, name, operands, in_specs, out_shapes, scratch):
    def whole(shape):
        return pl.BlockSpec(shape, lambda i: (0,) * len(shape))

    return pl.pallas_call(
        kernel,
        grid=(4,),
        in_specs=[pl.BlockSpec(memory_space=pltpu.SMEM)]
        + [pl.BlockSpec((2, 8 * ROWS, 2 * HD), lambda i: (i, 0, 0))] * 4
        + in_specs
        + [whole(o.shape) for o in operands[5 + len(in_specs) :]],
        out_specs=[whole(o.shape) for o in out_shapes],
        out_shape=out_shapes,
        scratch_shapes=[pltpu.VMEM((4, 2, 8 * ROWS, 2 * HD), BF16)] + scratch,
        cost_estimate=pl.CostEstimate(flops=1000, bytes_accessed=1000, transcendentals=0),
        compiler_params=params(1),
        name=name,
    )(*operands)


def early_weights(at, dqg, hid_a, grad_rows):
    return weights_call(
        early_weights_kernel,
        "early_weights",
        [at, *dqg, hid_a.reshape(8, 8, 16 * ROWS, HD), grad_rows.reshape(8, 8, 32 * ROWS, HD)],
        [
            pl.BlockSpec((8, 2, 16 * ROWS, HD), lambda i: (0, i, 0, 0)),
            pl.BlockSpec((8, 2, 32 * ROWS, HD), lambda i: (0, i, 0, 0)),
        ],
        [
            jax.ShapeDtypeStruct((8, HD, EPD * HD), F32),
            jax.ShapeDtypeStruct((8, EPD * HD, HD), F32),
        ],
        [],
    )


def late_weights(at, dqg, hid_b, wq, wo):
    (out,) = weights_call(
        late_weights_kernel,
        "late_weights",
        [at, *dqg, hid_b.reshape(8, 8, 16 * ROWS, HD), wq, wo],
        [pl.BlockSpec((8, 2, 16 * ROWS, HD), lambda i: (0, i, 0, 0))],
        [jax.ShapeDtypeStruct((8, EPD, 2, HD, HD), BF16)],
        [pltpu.VMEM((8, HD, EPD * HD), F32)],
    )
    return out


def projection_kernel(hid_ref, dkv_ref, out_ref):
    out_ref[...] = dot_tn(hid_ref[...], dkv_ref[...]).astype(BF16)


def projection(hid, dkv):
    return pl.pallas_call(
        projection_kernel,
        out_shape=jax.ShapeDtypeStruct((HD, 2 * HD), BF16),
        cost_estimate=pl.CostEstimate(flops=80000000000, bytes_accessed=1000, transcendentals=0),
        compiler_params=params(0),
        name="projection",
    )(hid, dkv)


def unpack_kernel(rho_ref, back_ref, swap_ref, out_ref, stage):
    for d in range(8):
        rows = back_ref[d * 8 : (d + 1) * 8, 0].reshape(64 * ROWS, HD)
        turned = dot_nn(swap_ref[...], rows).astype(BF16)
        for j in range(8):
            stage[j, d * 8 * ROWS : (d + 1) * 8 * ROWS, :] = turned[j * 8 * ROWS : (j + 1) * 8 * ROWS]
    row_id = lax.broadcasted_iota(jnp.int32, (64 * ROWS, BLOCK), 0)
    for j in range(8):
        x, span = j // 2, pl.ds((j % 2) * BLOCK, BLOCK)
        rho_a = rho_ref[x, 0, 0:1, span]
        rho_b = rho_ref[x, 0, 1:2, span]
        pick = ((row_id == rho_a) | (row_id == rho_b)).astype(F32).astype(BF16)
        out_ref[x, 0, span, :] = dot_tn(pick, stage[j])


def unpack(rho, back, swap):
    return pl.pallas_call(
        unpack_kernel,
        grid=(4,),
        in_specs=[
            pl.BlockSpec((4, 1, TOP, 2 * BLOCK), lambda t: (0, t, 0, 0)),
            pl.BlockSpec((64, 1, 8 * ROWS, HD), lambda t: (0, t, 0, 0)),
            pl.BlockSpec(swap.shape, lambda t: (0, 0)),
        ],
        out_specs=pl.BlockSpec((4, 1, 2 * BLOCK, HD), lambda t: (0, t, 0, 0)),
        out_shape=jax.ShapeDtypeStruct((4, 4, 2 * BLOCK, HD), F32),
        scratch_shapes=[pltpu.VMEM((8, 64 * ROWS, HD), BF16)],
        cost_estimate=pl.CostEstimate(flops=1000, bytes_accessed=1000, transcendentals=0),
        compiler_params=params(1),
        name="unpack_rows",
    )(rho, back, swap)


def finish_kernel(rows_ref, dkv_ref, wkv_ref, out_ref):
    for x in range(4):
        total = rows_ref[x, 0] + dot_nt(dkv_ref[x, 0], wkv_ref[...])
        out_ref[x, 0] = total.astype(BF16)


def finish(rows, dkv, wkv):
    return pl.pallas_call(
        finish_kernel,
        grid=(4,),
        in_specs=[
            pl.BlockSpec((4, 1, 2 * BLOCK, HD), lambda t: (0, t, 0, 0)),
            pl.BlockSpec((4, 1, 2 * BLOCK, 2 * HD), lambda t: (0, t, 0, 0)),
            pl.BlockSpec(wkv.shape, lambda t: (0, 0)),
        ],
        out_specs=pl.BlockSpec((4, 1, 2 * BLOCK, HD), lambda t: (0, t, 0, 0)),
        out_shape=jax.ShapeDtypeStruct((4, 4, 2 * BLOCK, HD), BF16),
        cost_estimate=pl.CostEstimate(flops=5000000000, bytes_accessed=10000000, transcendentals=0),
        compiler_params=params(1),
        name="finish_rows",
    )(rows, dkv, wkv)


def exchange(rows, axes):
    return lax.all_to_all(rows, axes, split_axis=0, concat_axis=0, tiled=True)


def shifted(rows, axis, s):
    n = lax.axis_size(axis)
    return lax.ppermute(rows, axis, [(i, (i + s) % n) for i in range(n)])


def gather(rows, axis):
    return [rows] + [shifted(rows, axis, s) for s in range(1, lax.axis_size(axis))]


def after(rows, *others):
    return lax.optimization_barrier((rows,) + others)[0]


def per_device(
    hidden, out_grad, queries, key_heads, value_heads, routes, route_gates, w_query, w_out, w_key, w_value
):
    swap, pad = swap_matrix().astype(BF16), pad_matrix().astype(BF16)
    unpad = pad.T
    xi, zh, zl = lax.axis_index("x"), lax.axis_index("zh"), lax.axis_index("zl")
    at = jnp.stack([xi, zh, zl])
    kv = lax.all_gather(jnp.concatenate([key_heads[0], value_heads[0]], axis=1), SEQ, axis=0, tiled=True)
    routes_t = routes[0].reshape(4, 4, 2 * BLOCK, TOP).transpose(0, 1, 3, 2)
    slab = (4, 4, 2 * BLOCK, HD)
    grad_packed, rho = pack(pack_first_kernel, routes_t, out_grad[0].reshape(slab), swap, 1, 0, 4)
    w_out_r = exchange(w_out, SLAB).reshape(8, EPD * HD, HD)
    grad_rows = exchange(after(grad_packed, w_out_r), WIDE)
    (hid_a,) = pack(pack_again_kernel, rho, hidden[0].reshape(slab), swap, 0, 0, 2)
    (hid_b,) = pack(pack_again_kernel, rho, hidden[0].reshape(slab), swap, 0, 2, 2)
    q = queries[0].transpose(1, 0, 2).reshape(TOP * BLOCK, HD)
    gates = route_gates[0].T.reshape(TOP * BLOCK, 1)
    own = lax.dynamic_slice(rho, (xi, zh, 0, zl * BLOCK), (1, 1, TOP, BLOCK)).reshape(TOP * BLOCK)
    own = own // ROWS * PAD + own % ROWS
    own_row, own_col = own.reshape(1, -1), own.reshape(-1, 1)

    parts = head_sums(after(grad_rows, own_row, own_col, q, gates, hid_a, hid_b), w_out_r)
    head_home = exchange(address_heads(parts, pad).reshape(256, PAD, HD), SEQ + GRP)
    hid_a = exchange(after(hid_a, head_home), WIDE)
    prob, head_out, gated = attend_forward(at, after(q, head_home), kv, gates)
    slots, dkv_part = attend_backward(
        head_home.reshape(256 * PAD, HD), own_row, own_col, gates, q, kv,
        prob, head_out, gated,
    )
    dkv_x = lax.psum_scatter(dkv_part, "x", scatter_dimension=0, tiled=True)
    mine = exchange(after(slots, hid_a).reshape(64, PAD, 2 * HD), WIDE).reshape(64 * PAD, 2 * HD)
    dqg = unpad_rows(mine, unpad).reshape(8, 8 * ROWS, 2 * HD)
    dqg = gather(dqg, "zh")
    w_query_r = exchange(after(w_query, mine), SLAB).reshape(8, EPD, HD, HD)
    dkv_z = exchange(after(dkv_x, w_query_r, *dqg).reshape(8, BLOCK, 2 * HD), ("zh", "zl"))
    dkv_own = dkv_z.astype(F32).sum(axis=0).astype(BF16)
    dkv = lax.all_gather(dkv_own, SEQ, axis=0, tiled=True)
    proj = projection(hidden[0], dkv)
    hid_b = exchange(after(hid_b, dkv_own), WIDE)
    wq, wo = early_weights(at, dqg, hid_a, grad_rows)
    back_rows = route_back(at, dqg, w_query_r).reshape(64, 4, 8 * ROWS, HD)
    back = exchange(after(back_rows, hid_b, wq), WIDE)
    dqg[0] = after(dqg[0], back_rows)
    grads = late_weights(at, dqg, hid_b, wq, wo).reshape(16, 2, HD, HD)
    grads = exchange(after(grads, back, proj), SLAB)
    grad_wq, grad_wo = grads[:, 0].astype(F32), grads[:, 1].astype(F32)

    wkv = jnp.concatenate([w_key, w_value], axis=1)
    unpacked = unpack(rho, after(back, proj), swap)
    grad_hidden = finish(unpacked, dkv.reshape(4, 4, 2 * BLOCK, 2 * HD), wkv).reshape(1, 4096, HD)
    proj = sum(p.astype(F32) for p in gather(proj, "dev")).astype(BF16)
    proj = [p.astype(F32) for p in gather(proj, "node")]
    proj[0] = after(proj[0], grad_hidden)
    proj = (proj[0] + proj[2]) + (proj[1] + proj[3])
    return (grad_hidden, grad_wq, grad_wo, proj[:, :HD], proj[:, HD:])


def solution(mesh):
    fine = Mesh(mesh.devices.reshape(4, 4, 2, 4, 2), SEQ + GRP)
    in_specs = (
        P(GRP, None, SEQ),
        P(GRP, None, SEQ),
        P(GRP, SEQ, None, None),
        P(GRP, SEQ, None),
        P(GRP, SEQ, None),
        P(GRP, None, None),
        P(GRP, SEQ, None),
        P(GRP, SEQ, None),
        P(GRP, None, SEQ),
        P(SEQ, None),
        P(SEQ, None),
    )
    out_specs = (
        P(GRP, None, SEQ),
        P(GRP, SEQ, None),
        P(GRP, None, SEQ),
        P(SEQ, None),
        P(SEQ, None),
    )
    return jax.shard_map(per_device, mesh=fine, in_specs=in_specs, out_specs=out_specs, check_vma=False)
```
